256 devices in a mesh: curve: 64 (over z_hi, x, y, core), lev: 4 (over z_lo).
Axes of the slice: x: 4, y: 4, z: 8 (z_hi: 2, z_lo: 4; z = z_hi * 4 + z_lo), core: 2. Of those that a mesh axis runs over, the one named last changes fastest.
Arguments:
- state: float32 [128, 16, 24576], P('lev', None, 'curve'), may hold values from -6 to 6
- wind_x: float32 [128, 16, 24576], P('lev', None, 'curve'), may hold values from -6 to 6
- wind_y: float32 [128, 16, 24576], P('lev', None, 'curve'), may hold values from -6 to 6
- neighbor: int32 [4, 24576], P(None, 'curve'), may hold values from 0 to 24575, as said below
- neighbor_edge: int32 [4, 24576], P(None, 'curve'), may hold values from 0 to 3
- reversed_edge: int32 [4, 24576], P(None, 'curve'), may hold values from 0 to 1
- branch_mask: int32 [16, 24576], P('lev', 'curve'), may hold values from 0 to 1, as said below
- mixing: float32 [128, 128], replicated, may hold values from -0.5 to 0.5
Outputs:
- updated: float32 [128, 16, 24576], P('lev', None, 'curve')
The draws below stay inside these ranges and needn't reach their ends.
Inputs may be any that keep to these rules, and one draw needn't show every extreme that they name: Elements are numbered face by face over the six faces of a cube of 64 x 64 elements a face: element f * 64 * 64 + 64 * r + q lies on face f in row r and column c, with c = q for even r and c = 63 - q for odd r. Across edge 0 lies row r - 1, across edge 1 column c + 1, across edge 2 row r + 1, across edge 3 column c - 1 of the same face where that row or column exists; otherwise the element across lies on another face. Row 0 of face 3 borders row 63 of face 2 (across its edge 0). The tables are mutual: element neighbor[k, e] has e across its edge neighbor_edge[k, e], with the same reversed_edge. `branch_mask`: take the block of points of one lev index (16 / 4 consecutive points) and elements of one curve index: at most 1152 of its 1536 columns are 1, and for every lev index some block has exactly 1152.
All inputs are finite; a program needn't handle non-finite values.
Results may differ from the reference program's by a relative error of at most 0.0001.
Values sent between devices are 32-bit elements; how exact they have to be, the bound alone decides.
No kernel may reach another device: no remote copies, remote signals or barrier semaphores. Data moves between devices by JAX's collectives and lax.ppermute only.
A program may use at most 64 MiB of HBM per device.

```python
import math
import jax
import jax.numpy as jnp
import numpy as np
from jax import lax

NE = 64
LEV = 128
NPTS = 16
ELEMS = 24576
E_DEV = 384
COLS_LEV = 1536
MAXM = 1152
N_CURVE = 64
N_LEV = 4


def cube_tables(key):
    order_key, frame_key, flip_key = jax.random.split(key, 3)
    order = jax.random.permutation(order_key, 6).astype(jnp.int32)
    frames = jax.random.randint(frame_key, (6,), 0, 8).astype(jnp.int32)
    flip = jax.random.randint(flip_key, (), 0, 2).astype(jnp.int32)
    frames = frames.at[0].set(0).at[2].set(2 + flip)
    faces = jnp.arange(6, dtype=jnp.int32)
    third = order[2]
    third_axis = third // 2
    third_side = third % 2
    third_frame = frames[third]
    third_swapped = third_frame // 4
    third_sign = 1 - 2 * (third_frame // 2 % 2)
    third_axis_b = jnp.where(third_swapped == 1, (third_axis + 2) % 3, (third_axis + 1) % 3)
    fourth = 2 * third_axis_b + jnp.where(third_sign > 0, 1, 0)
    holder = jnp.sum(jnp.where(order == fourth, faces, 0))
    order = order.at[holder].set(order[3]).at[3].set(fourth)
    fourth_axis = fourth // 2
    fourth_swapped = jnp.where((fourth_axis + 1) % 3 == third_axis, 0, 1)
    frames = frames.at[fourth].set(4 * fourth_swapped + 2 * third_side + frames[fourth] % 2)
    span = 2 * NE
    axis_a = faces // 2
    side = faces % 2
    swapped = frames // 4
    sign_a = 1 - 2 * (frames // 2 % 2)
    sign_b = 1 - 2 * (frames % 2)
    axis_b = jnp.where(swapped == 1, (axis_a + 2) % 3, (axis_a + 1) % 3)
    axis_c = 3 - axis_a - axis_b
    unit = jnp.eye(3, dtype=jnp.int32)
    normal = (2 * side - 1)[:, None] * unit[axis_a]
    vec_a = sign_a[:, None] * unit[axis_b]
    vec_b = sign_b[:, None] * unit[axis_c]
    anchor = (side * span)[:, None] * unit[axis_a]
    anchor = anchor + jnp.where(sign_a < 0, span, 0)[:, None] * unit[axis_b]
    anchor = anchor + jnp.where(sign_b < 0, span, 0)[:, None] * unit[axis_c]
    cells = NE * NE
    index = jnp.arange(ELEMS, dtype=jnp.int32)
    face_slot = index // cells
    within = index % cells
    row_index = within // NE
    raw_col = within % NE
    column = jnp.where(row_index % 2 == 0, raw_col, NE - 1 - raw_col)
    face = order[face_slot]
    along_a = vec_a[face]
    along_b = vec_b[face]
    center = anchor[face] + (2 * row_index + 1)[:, None] * along_a + (2 * column + 1)[:, None] * along_b
    outward = jnp.stack([-along_a, along_b, along_a, -along_b])
    crossing = jnp.stack([row_index == 0, column == NE - 1, row_index == NE - 1, column == 0])
    middle = center[None] + outward
    target = jnp.where(crossing[:, :, None], middle - normal[face][None], center[None] + 2 * outward)
    axes_ids = jnp.arange(3, dtype=jnp.int32)
    other_face = jnp.sum(jnp.where(target == 0, 2 * axes_ids, 0) + jnp.where(target == span, 2 * axes_ids + 1, 0), axis=2)
    relative = target - anchor[other_face]
    other_a = vec_a[other_face]
    other_b = vec_b[other_face]
    other_row = (jnp.sum(relative * other_a, axis=2) - 1) // 2
    other_col = (jnp.sum(relative * other_b, axis=2) - 1) // 2
    inverse = jnp.zeros(6, jnp.int32).at[order].set(faces)
    other_slot = inverse[other_face]
    other_raw = jnp.where(other_row % 2 == 0, other_col, NE - 1 - other_col)
    neighbor = other_slot * cells + other_row * NE + other_raw
    toward = middle - target
    candidates = jnp.stack([-other_a, other_b, other_a, -other_b])
    matches = jnp.all(candidates == toward[None], axis=3)
    edge_ids = jnp.arange(4, dtype=jnp.int32)[:, None, None]
    neighbor_edge = jnp.sum(jnp.where(matches, edge_ids, 0), axis=0)
    own_dir = jnp.stack([along_b, along_a, along_b, along_a])
    their_dir = jnp.where((neighbor_edge % 2 == 0)[:, :, None], other_b, other_a)
    reversed_edge = (jnp.sum(own_dir * their_dir, axis=2) < 0).astype(jnp.int32)
    return (neighbor.astype(jnp.int32), neighbor_edge.astype(jnp.int32), reversed_edge)


def draw_neighbor(key, part):
    tables = cube_tables(key)
    return tables[0]


def draw_neighbor_edge(key, part):
    tables = cube_tables(key)
    return tables[1]


def draw_reversed_edge(key, part):
    tables = cube_tables(key)
    return tables[2]


def draw_branch_mask(key, part):
    key = jax.random.fold_in(key, 23)
    count_key, pick_key, score_key = jax.random.split(key, 3)
    counts = jax.random.randint(count_key, (N_LEV, N_CURVE), COLS_LEV // 8, MAXM + 1)
    pick = jax.random.randint(pick_key, (N_LEV, 1), 0, N_CURVE)
    counts = jnp.where(jnp.arange(N_CURVE)[None, :] == pick, MAXM, counts)
    scores = jax.random.randint(score_key, (N_LEV, N_CURVE, COLS_LEV), 0, 1 << 16)
    scores = scores * COLS_LEV + jnp.arange(COLS_LEV)[None, None, :]
    ranks = jnp.argsort(jnp.argsort(scores, axis=2, stable=True), axis=2, stable=True)
    marked = (ranks < counts[:, :, None]).astype(jnp.int32)
    per_block = 16 // N_LEV
    marked = marked.reshape(N_LEV, N_CURVE, per_block, E_DEV).transpose(0, 2, 1, 3)
    return marked.reshape(16, ELEMS).astype(jnp.int32)


def shard_levels(rng, dims, cuts, smallest, top_value):
    factor_of, own = 1.0, jax.random.fold_in(rng, 6)
    for axis_at, shards_of in cuts:
        steps = jnp.exp(jax.random.uniform(jax.random.fold_in(own, axis_at), (shards_of,), jnp.float32, smallest / len(cuts), top_value / len(cuts)))
        factor_of = factor_of * jnp.repeat(steps, dims[axis_at] // shards_of).reshape([-1 if axis == axis_at else 1 for axis in range(len(dims))])
    return factor_of


def centred(key, extent, spread, reach, cuts=(), held_as=jnp.bfloat16):
    values = spread * jax.random.normal(key, extent, jnp.float32)
    if cuts:
        values = values * shard_levels(key, extent, cuts, -0.22, 0.18)
    return jnp.clip(values, -reach, reach).astype(held_as)


def setup_inputs(seed: int = 0) -> dict:
    seeds = jax.random.split(jax.random.key(seed), 9)
    state = centred(seeds[0], (LEV, NPTS, ELEMS), 1.0, 6.0, ((0, 4), (2, 64)), jnp.float32)
    wind_x = centred(seeds[1], (LEV, NPTS, ELEMS), 1.0, 6.0, ((0, 4), (2, 64)), jnp.float32)
    wind_y = centred(seeds[2], (LEV, NPTS, ELEMS), 1.0, 6.0, ((0, 4), (2, 64)), jnp.float32)
    neighbor = draw_neighbor(jax.random.fold_in(seeds[8], 71), 0)
    neighbor_edge = draw_neighbor_edge(jax.random.fold_in(seeds[8], 71), 0)
    reversed_edge = draw_reversed_edge(jax.random.fold_in(seeds[8], 71), 0)
    branch_mask = draw_branch_mask(jax.random.fold_in(seeds[8], 71), 0)
    mixing = centred(seeds[7], (LEV, LEV), LEV ** -0.5, 0.5, (), jnp.float32)
    return {"state": state, "wind_x": wind_x, "wind_y": wind_y, "neighbor": neighbor, "neighbor_edge": neighbor_edge, "reversed_edge": reversed_edge, "branch_mask": branch_mask, "mixing": mixing}


def derivative_table():
    nodes = np.array([-1.0, -1.0 / math.sqrt(5.0), 1.0 / math.sqrt(5.0), 1.0])
    weights = np.array([1.0 / np.prod([nodes[j] - nodes[m] for m in range(4) if m != j]) for j in range(4)])
    table = np.zeros((4, 4))
    for i in range(4):
        for j in range(4):
            if i == j:
                table[i, j] = sum((1.0 / (nodes[i] - nodes[m]) for m in range(4) if m != i))
            else:
                table[i, j] = weights[j] / weights[i] / (nodes[i] - nodes[j])
    return table

def slot_table():
    table = np.zeros((16, 16))
    for t in range(4):
        table[0 * 4 + t, 0 * 4 + t] = 1.0
        table[1 * 4 + t, t * 4 + 3] = 1.0
        table[2 * 4 + t, 3 * 4 + t] = 1.0
        table[3 * 4 + t, t * 4 + 0] = 1.0
    return table

def reference(state, wind_x, wind_y, neighbor, neighbor_edge, reversed_edge, branch_mask, mixing):
    high = lax.Precision.HIGHEST
    deriv = jnp.asarray(derivative_table(), jnp.float32)
    slots = jnp.asarray(slot_table(), jnp.float32)
    grid = state.reshape(LEV, 4, 4, ELEMS)
    dxi = jnp.einsum('ai,lije->laje', deriv, grid, precision=high).reshape(LEV, 16, ELEMS)
    deta = jnp.einsum('bj,lije->libe', deriv, grid, precision=high).reshape(LEV, 16, ELEMS)
    stepped = state - 0.05 * (wind_x * dxi + wind_y * deta)
    own = jnp.einsum('sg,lge->lse', slots, stepped, precision=high)
    position = jnp.arange(4, dtype=jnp.int32)
    source_pos = jnp.where(reversed_edge[:, None, :] == 1, 3 - position[None, :, None], position[None, :, None])
    source_slot = (neighbor_edge[:, None, :] * 4 + source_pos).reshape(16, ELEMS)
    source_elem = jnp.broadcast_to(neighbor[:, None, :], (4, 4, ELEMS)).reshape(16, ELEMS)
    flat_index = (source_slot * ELEMS + source_elem).reshape(-1).astype(jnp.int32)
    across = jnp.take(own.reshape(LEV, 16 * ELEMS), flat_index, axis=1).reshape(LEV, 16, ELEMS)
    dynamics = stepped + 0.5 * jnp.einsum('sg,lse->lge', slots, across - own, precision=high)
    columns = state.reshape(LEV, 16 * ELEMS)
    mixed = jnp.dot(mixing, columns, precision=high, preferred_element_type=jnp.float32)
    heavy = 0.5 * jnp.tanh(mixed) - 0.25 * columns
    plain = -0.3 * columns / (1.0 + columns * columns)
    marked = branch_mask.reshape(1, 16 * ELEMS) == 1
    increment = jnp.where(marked, heavy, plain).reshape(LEV, 16, ELEMS)
    return dynamics + increment
```

```python
import functools
import math

import jax
import jax.numpy as jnp
import numpy as np
from jax import lax
from jax.experimental import pallas as pl
from jax.experimental.pallas import tpu as pltpu
from jax.sharding import PartitionSpec as P

NE = 64
ROWS = 6
E = ROWS * NE
CONTRIB = 144
MERGED = 176
PIECE = 2 * MERGED
SIDE = 4 * PIECE
VMEM = pl.BlockSpec(memory_space=pltpu.VMEM)
LIMIT = 48 * 1024 * 1024
NT = (((1,), (1,)), ((), ()))
TN = (((0,), (0,)), ((), ()))


def derivative_table():
    nodes = np.array([-1.0, -1.0 / math.sqrt(5.0), 1.0 / math.sqrt(5.0), 1.0])
    weights = np.array(
        [1.0 / np.prod([nodes[j] - nodes[m] for m in range(4) if m != j]) for j in range(4)]
    )
    table = np.zeros((4, 4))
    for i in range(4):
        for j in range(4):
            if i == j:
                table[i, j] = sum((1.0 / (nodes[i] - nodes[m]) for m in range(4) if m != i))
            else:
                table[i, j] = weights[j] / weights[i] / (nodes[i] - nodes[j])
    table[1, 1] = table[2, 2] = 0.0
    return table


DERIV = derivative_table()


def f32(shape):
    return jax.ShapeDtypeStruct(shape, jnp.float32)


def call(kernel, out_shape, n_in, scratch=()):
    return pl.pallas_call(
        kernel,
        out_shape=out_shape,
        in_specs=[VMEM] * n_in,
        out_specs=jax.tree.map(lambda _: VMEM, out_shape),
        scratch_shapes=list(scratch),
        compiler_params=pltpu.CompilerParams(vmem_limit_bytes=LIMIT),
    )


def lane_blocks(*leading):
    return pl.BlockSpec((*leading, 128), lambda c: (0,) * len(leading) + (c,))


def whole(*shape):
    return pl.BlockSpec(shape, lambda c: (0,) * len(shape))


def lane_call(kernel, out_shape, in_specs, out_specs):
    return pl.pallas_call(
        kernel,
        grid=(3,),
        out_shape=out_shape,
        in_specs=in_specs,
        out_specs=out_specs,
        compiler_params=pltpu.CompilerParams(vmem_limit_bytes=LIMIT),
    )


def split_kernel(state, *sends):
    me = lax.axis_index("lev")
    for k in range(4):
        first = 4 * lax.rem(me + k, 4)
        for p in range(4):
            sends[k][p] = state[pl.ds(first + p, 32, stride=16), :]


def rim_rows():
    start = lax.axis_index("curve") * ROWS
    return (NE - lax.rem(start, NE)) % NE, NE - 1 - lax.rem(start, NE)


def exact_dot(selector, values, dims):
    high = values.astype(jnp.bfloat16)
    rest = values - high.astype(jnp.float32)
    middle = rest.astype(jnp.bfloat16)
    low = (rest - middle.astype(jnp.float32)).astype(jnp.bfloat16)
    out = None
    for part in (low, middle, high):
        args = (selector, part) if dims == NT else (part, selector)
        term = lax.dot_general(*args, dims, preferred_element_type=jnp.float32)
        out = term if out is None else out + term
    return out


def step_kernel(state, wind_x, wind_y, stepped, contrib, last, first):
    step = pl.program_id(0)
    lanes = pl.ds(pl.multiple_of(128 * step, 128), 128)
    for tile in range(4):
        at = [pl.ds(128 * tile + p, 8, stride=16) for p in range(16)]
        x = [state[at[p], :] for p in range(16)]
        for a in range(4):
            for b in range(4):
                p = 4 * a + b
                dxi = sum(float(DERIV[a, i]) * x[4 * i + b] for i in range(4) if DERIV[a, i])
                deta = sum(float(DERIV[b, j]) * x[4 * a + j] for j in range(4) if DERIV[b, j])
                moved = wind_x[at[p], :] * dxi + wind_y[at[p], :] * deta
                stepped[p, 8 * tile : 8 * tile + 8, lanes] = x[p] - 0.05 * moved

    @pl.when(step == 2)
    def _():
        take_edges(stepped, contrib, last, first)


def take_edges(stepped, contrib, last, first):
    edge = [
        stepped[0:4].reshape(128, E),
        jnp.concatenate([stepped[4 * t + 3] for t in range(4)], axis=0),
        stepped[12:16].reshape(128, E),
        jnp.concatenate([stepped[4 * t] for t in range(4)], axis=0),
    ]
    last[...] = edge[2][:, 256:]
    first[...] = edge[0][:, :128]
    row0, row63 = rim_rows()
    r = lax.broadcasted_iota(jnp.int32, (8, E), 0)
    lane = lax.broadcasted_iota(jnp.int32, (8, E), 1)
    odd = r % 2
    left = ((lane == NE * r + (NE - 1) * odd) & (r < ROWS)).astype(jnp.bfloat16)
    right = ((lane == NE * r + (NE - 1) * (1 - odd)) & (r < ROWS)).astype(jnp.bfloat16)
    contrib[0:6] = exact_dot(left, edge[3], NT)[0:6]
    contrib[6:12] = exact_dot(right, edge[1], NT)[0:6]
    r = lax.broadcasted_iota(jnp.int32, (NE, E), 0)
    lane = lax.broadcasted_iota(jnp.int32, (NE, E), 1)
    contrib[12:76] = exact_dot((lane == NE * row0 + r).astype(jnp.bfloat16), edge[0], NT)
    contrib[76:140] = exact_dot((lane == NE * row63 + r).astype(jnp.bfloat16), edge[2], NT)
    contrib[140:144] = jnp.zeros((4, 128), jnp.float32)


def merge_kernel(a, b, c, d, out):
    for k, part in enumerate((a, b, c, d)):
        out[12 * k : 12 * k + 12] = part[0:12]
    out[48:176] = (a[12:140] + b[12:140]) + (c[12:140] + d[12:140])


def physics_kernel(own, one, two, three, mask, mixing, *rest):
    backs, (columns, change) = rest[:4], rest[4:]
    me = lax.axis_index("lev")
    rows = [pl.ds(pl.multiple_of(32 * lax.rem(me + 4 - k, 4), 32), 32) for k in range(4)]
    mix = mixing[...]
    for p in range(4):
        for k, part in enumerate((own, one, two, three)):
            columns[p, rows[k], :] = part[p]
        x = columns[p]
        mixed = lax.dot_general(
            mix,
            x,
            (((1,), (0,)), ((), ())),
            precision=lax.Precision.HIGHEST,
            preferred_element_type=jnp.float32,
        )
        heavy = 0.5 * jnp.tanh(mixed) - 0.25 * x
        plain = -0.3 * x / (1.0 + x * x)
        change[p] = jnp.where(mask[p : p + 1, :] == 1, heavy, plain)
        for k in range(4):
            backs[k][p] = change[p, rows[k], :]


def edge_kernel(
    stepped, before, after, pool_own, pool_other, neighbor, neighbor_edge, reversed_edge, dynamics
):
    curve = lax.axis_index("curve")
    row0, row63 = rim_rows()
    my_z, my_x, my_y, my_c = curve // 32, (curve // 8) % 4, (curve // 2) % 4, curve % 2
    near, edge_of = neighbor[...], neighbor_edge[...]
    turned = reversed_edge[...] == 1
    device = ((near // 128) * 171) // 512
    lane_of = near - E * device
    row_of, along = lane_of // NE, lane_of % NE
    k_z = (device // 32 + my_z) % 2
    k_x = (my_x + 4 - (device // 8) % 4) % 4
    k_y = (my_y + 4 - (device // 2) % 4) % 4
    k_c = (device + my_c) % 2
    in_piece = jnp.where(
        edge_of % 2 == 1,
        12 * k_y + jnp.where(edge_of == 3, 0, 6) + row_of,
        48 + jnp.where(edge_of == 0, 0, NE) + along,
    )
    place = SIDE * k_c + PIECE * k_x + MERGED * k_z + in_piece
    lane = lax.broadcasted_iota(jnp.int32, (1, 128), 1)
    half = lane // NE
    side_lane = (lane % NE == 0) | (lane % NE == NE - 1)
    at_left = (lane == 0) | (lane == 127)

    def row_place(k, row):
        picked = [
            jnp.where(row // 2 == v, place[k : k + 1, 128 * v : 128 * v + 128], 0) for v in range(3)
        ]
        return picked[0] + picked[1] + picked[2]

    sides = jnp.zeros((1, 128), jnp.int32)
    for v in range(3):
        lanes = slice(128 * v, 128 * v + 128)
        both = jnp.where(at_left, place[3:4, lanes], place[1:2, lanes])
        both = jnp.where(side_lane, both, 0)
        sides = sides + (pltpu.roll(both, 2 * v, 1) if v else both)
    wanted = jnp.concatenate([row_place(0, row0), row_place(2, row63), sides], axis=1)
    found = None
    for k, pool in enumerate((pool_own, pool_other)):
        at = lax.broadcasted_iota(jnp.int32, (SIDE, 3 * 128), 0) + SIDE * k
        part = exact_dot((at == wanted).astype(jnp.bfloat16), pool[...], TN)
        found = part if found is None else found + part
    found0, found2, found_side = found[:, :128], found[:, 128:256], found[:, 256:]

    backwards = 127 - lax.broadcasted_iota(jnp.int32, (128, 128), 1)

    def flip(values):
        return jnp.take_along_axis(values, backwards, axis=1)

    def oriented(values, turn):
        four = [values[32 * t : 32 * t + 32] for t in range(4)]
        return [jnp.where(turn, four[3 - t], four[t]) for t in range(4)]

    point = [
        [0, 1, 2, 3],
        [3, 7, 11, 15],
        [12, 13, 14, 15],
        [0, 4, 8, 12],
    ]

    def edge(k, v):
        return jnp.concatenate(
            [stepped[p, :, 128 * v : 128 * v + 128] for p in point[k]], axis=0
        )

    flipped0 = [flip(edge(0, v)) for v in range(3)] + [flip(after[...])]
    flipped2 = [flip(before[...])] + [flip(edge(2, v)) for v in range(3)]
    lower = half == 0
    for v in range(3):
        lanes = slice(128 * v, 128 * v + 128)
        row = 2 * v + half
        own = [edge(k, v) for k in range(4)]
        back = pltpu.roll(found_side, (128 - 2 * v) % 128, 1) if v else found_side
        to_next = [pltpu.roll(own[k], 127, 1) for k in (1, 3)]
        to_last = [pltpu.roll(own[k], 1, 1) for k in (1, 3)]
        across = [
            jnp.where(lower, flipped2[v], flipped2[v + 1]),
            jnp.where(lower, to_next[1], to_last[1]),
            jnp.where(lower, flipped0[v], flipped0[v + 1]),
            jnp.where(lower, to_last[0], to_next[0]),
        ]
        across[0] = jnp.where(row == row0, found0, across[0])
        across[2] = jnp.where(row == row63, found2, across[2])
        across[3] = jnp.where(at_left, back, across[3])
        across[1] = jnp.where(side_lane & ~at_left, back, across[1])
        total = [stepped[p, :, lanes] for p in range(16)]
        for k in range(4):
            theirs = oriented(across[k], turned[k : k + 1, lanes])
            for t in range(4):
                p = point[k][t]
                total[p] = total[p] + 0.5 * (theirs[t] - own[k][32 * t : 32 * t + 32])
        for p in range(16):
            dynamics[p, :, lanes] = total[p]


def add_kernel(dynamics, own, one, two, three, out):
    me = lax.axis_index("lev")
    for k, part in enumerate((own, one, two, three)):
        first = 4 * lax.rem(me + k, 4)
        for p in range(4):
            out[pl.ds(first + p, 32, stride=16), :] = dynamics[first + p] + part[p]


def on_device(state, wind_x, wind_y, neighbor, neighbor_edge, reversed_edge, branch_mask, mixing):
    flat = state.reshape(512, E)
    part = f32((4, 32, E))
    flat_block, part_block = lane_blocks(512), lane_blocks(4, 32)
    sends = lane_call(split_kernel, (part,) * 4, [flat_block], (part_block,) * 4)(flat)
    cells = [
        lax.ppermute(sends[k], "lev", [(i, (i + k) % 4) for i in range(4)]) for k in (1, 2, 3)
    ]
    stepped, contrib, last, first = lane_call(
        step_kernel,
        (f32((16, 32, E)), f32((CONTRIB, 128)), f32((128, 128)), f32((128, 128))),
        [flat_block] * 3,
        (whole(16, 32, E), whole(CONTRIB, 128), whole(128, 128), whole(128, 128)),
    )(flat, wind_x.reshape(512, E), wind_y.reshape(512, E))
    before = lax.ppermute(last, "curve", [(i, i + 1) for i in range(63)])
    after = lax.ppermute(first, "curve", [(i + 1, i) for i in range(63)])

    def turn(shift, k):
        def to(i):
            return (i & ~(3 << shift)) | ((((i >> shift) + k) & 3) << shift)

        return [(i, to(i)) for i in range(64)]

    along_y = [lax.ppermute(contrib, "curve", turn(1, k)) for k in (1, 2, 3)]
    merged = call(merge_kernel, f32((MERGED, 128)), 4)(contrib, *along_y)
    other_z = lax.ppermute(merged, "curve", [(i, i ^ 32) for i in range(64)])
    piece = jnp.concatenate([merged, other_z], axis=0)
    along_x = [lax.ppermute(piece, "curve", turn(3, k)) for k in (1, 2, 3)]
    pool = jnp.concatenate([piece, *along_x], axis=0)
    pool_other = lax.ppermute(pool, "curve", [(i, i ^ 1) for i in range(64)])

    backs = call(
        physics_kernel,
        (part,) * 4,
        6,
        [pltpu.VMEM((4, 128, E), jnp.float32), pltpu.VMEM((4, 128, E), jnp.float32)],
    )(sends[0], *cells, branch_mask, mixing)
    changes = [
        lax.ppermute(backs[k], "lev", [(i, (i - k) % 4) for i in range(4)]) for k in (1, 2, 3)
    ]
    dynamics = call(edge_kernel, f32((16, 32, E)), 8)(
        stepped, before, after, pool, pool_other, neighbor, neighbor_edge, reversed_edge
    )
    out = lane_call(
        add_kernel, f32((512, E)), [lane_blocks(16, 32)] + [part_block] * 4, flat_block
    )(dynamics, backs[0], *changes)
    return out.reshape(32, 16, E)


def solution(mesh):
    in_specs = (
        P("lev", None, "curve"),
        P("lev", None, "curve"),
        P("lev", None, "curve"),
        P(None, "curve"),
        P(None, "curve"),
        P(None, "curve"),
        P("lev", "curve"),
        P(),
    )
    out_specs = P("lev", None, "curve")
    return jax.shard_map(
        on_device, mesh=mesh, in_specs=in_specs, out_specs=out_specs, check_vma=False
    )
```

```python
import functools
import math

import jax
import jax.numpy as jnp
import numpy as np
from jax import lax
from jax.experimental import pallas as pl
from jax.experimental.pallas import tpu as pltpu
from jax.sharding import PartitionSpec as P

NE = 64
ROWS = 6
E = ROWS * NE
CONTRIB = 144
PAIRED = 152
MERGED = 224
PIECE = 2 * MERGED
VMEM = pl.BlockSpec(memory_space=pltpu.VMEM)
ANY = pl.BlockSpec(memory_space=pl.ANY)
LIMIT = 24 * 1024 * 1024
NT = (((1,), (1,)), ((), ()))
TN = (((0,), (0,)), ((), ()))


def derivative_table():
    nodes = np.array([-1.0, -1.0 / math.sqrt(5.0), 1.0 / math.sqrt(5.0), 1.0])
    weights = np.array(
        [1.0 / np.prod([nodes[j] - nodes[m] for m in range(4) if m != j]) for j in range(4)]
    )
    table = np.zeros((4, 4))
    for i in range(4):
        for j in range(4):
            if i == j:
                table[i, j] = sum((1.0 / (nodes[i] - nodes[m]) for m in range(4) if m != i))
            else:
                table[i, j] = weights[j] / weights[i] / (nodes[i] - nodes[j])
    table[1, 1] = table[2, 2] = 0.0
    return table


DERIV = derivative_table()


def f32(shape):
    return jax.ShapeDtypeStruct(shape, jnp.float32)


def call(kernel, out_shape, n_in, scratch=(), out_spec=VMEM, cost=None):
    return pl.pallas_call(
        kernel,
        out_shape=out_shape,
        in_specs=[VMEM] * n_in,
        out_specs=jax.tree.map(lambda _: out_spec, out_shape),
        scratch_shapes=list(scratch),
        compiler_params=pltpu.CompilerParams(vmem_limit_bytes=LIMIT),
        cost_estimate=cost,
    )


def lane_blocks(*leading):
    return pl.BlockSpec((*leading, 128), lambda c: (0,) * len(leading) + (c,))


def whole(*shape):
    return pl.BlockSpec(shape, lambda c: (0,) * len(shape))


def lane_call(kernel, out_shape, in_specs, out_specs):
    return pl.pallas_call(
        kernel,
        grid=(3,),
        out_shape=out_shape,
        in_specs=in_specs,
        out_specs=out_specs,
        compiler_params=pltpu.CompilerParams(vmem_limit_bytes=LIMIT),
    )


def split_kernel(state, *sends):
    me = lax.axis_index("lev")
    for k in range(4):
        first = 4 * (me ^ k)
        for p in range(4):
            sends[k][p] = state[pl.ds(first + p, 32, stride=16), :]


def rim_rows():
    start = lax.axis_index("curve") * ROWS
    return (NE - lax.rem(start, NE)) % NE, NE - 1 - lax.rem(start, NE)


def exact_dot(selector, values, dims):
    high = values.astype(jnp.bfloat16)
    rest = values - high.astype(jnp.float32)
    middle = rest.astype(jnp.bfloat16)
    low = (rest - middle.astype(jnp.float32)).astype(jnp.bfloat16)
    out = None
    for part in (low, middle, high):
        args = (selector, part) if dims == NT else (part, selector)
        term = lax.dot_general(*args, dims, preferred_element_type=jnp.float32)
        out = term if out is None else out + term
    return out


def step_kernel(
    state,
    wind_x,
    wind_y,
    _sent,
    near,
    edge_of,
    stepped,
    contrib,
    to_partner,
    to_other,
    wanted,
):
    step = pl.program_id(0)
    lanes = pl.ds(pl.multiple_of(128 * step, 128), 128)
    for tile in range(4):
        at = [pl.ds(128 * tile + p, 8, stride=16) for p in range(16)]
        x = [state[at[p], :] for p in range(16)]
        for a in range(4):
            for b in range(4):
                p = 4 * a + b
                dxi = sum(float(DERIV[a, i]) * x[4 * i + b] for i in range(4) if DERIV[a, i])
                deta = sum(float(DERIV[b, j]) * x[4 * a + j] for j in range(4) if DERIV[b, j])
                moved = wind_x[at[p], :] * dxi + wind_y[at[p], :] * deta
                stepped[p, 8 * tile : 8 * tile + 8, lanes] = x[p] - 0.05 * moved

    @pl.when(step == 2)
    def _():
        take_edges(stepped, contrib, to_partner, to_other)
        wanted[...] = wanted_places(near[...], edge_of[...])


def take_edges(stepped, contrib, to_partner, to_other):
    edge = [
        stepped[0:4].reshape(128, E),
        jnp.concatenate([stepped[4 * t + 3] for t in range(4)], axis=0),
        stepped[12:16].reshape(128, E),
        jnp.concatenate([stepped[4 * t] for t in range(4)], axis=0),
    ]
    last, first = edge[2][:, 256:], edge[0][:, :128]
    low = lax.broadcasted_iota(jnp.int32, (64, 128), 1) < NE
    last = jnp.where(low, pltpu.roll(last[:64], NE, 1), last[64:])
    first = jnp.where(low, first[:64], pltpu.roll(first[64:], NE, 1))
    even = lax.axis_index("curve") % 2 == 0
    to_partner[...] = jnp.where(even, last, first)
    to_other[...] = jnp.where(even, first, last)
    row0, row63 = rim_rows()
    r = lax.broadcasted_iota(jnp.int32, (8, E), 0)
    lane = lax.broadcasted_iota(jnp.int32, (8, E), 1)
    odd = r % 2
    left = ((lane == NE * r + (NE - 1) * odd) & (r < ROWS)).astype(jnp.bfloat16)
    right = ((lane == NE * r + (NE - 1) * (1 - odd)) & (r < ROWS)).astype(jnp.bfloat16)
    contrib[0:6] = exact_dot(left, edge[3], NT)[0:6]
    contrib[6:12] = exact_dot(right, edge[1], NT)[0:6]
    r = lax.broadcasted_iota(jnp.int32, (NE, E), 0)
    lane = lax.broadcasted_iota(jnp.int32, (NE, E), 1)
    contrib[12:76] = exact_dot((lane == NE * row0 + r).astype(jnp.bfloat16), edge[0], NT)
    contrib[76:140] = exact_dot((lane == NE * row63 + r).astype(jnp.bfloat16), edge[2], NT)
    contrib[140:CONTRIB] = jnp.zeros((CONTRIB - 140, 128), jnp.float32)


def pair_kernel(a, b, _row, out):
    out[0:12] = a[0:12]
    out[12:24] = b[0:12]
    out[24:152] = a[12:140] + b[12:140]


def merge_kernel(a, b, c, d, out, done):
    for k, part in enumerate((a, b, c, d)):
        out[24 * k : 24 * k + 24] = part[0:24]
    out[96:224] = (a[24:152] + b[24:152]) + (c[24:152] + d[24:152])
    done[...] = jnp.zeros((8, 128), jnp.float32)


def join_kernel(mine, theirs, partner_row, other_row, out, before, after):
    out[:MERGED] = mine[...]
    out[MERGED:] = theirs[...]
    even = lax.axis_index("curve") % 2 == 0
    partner, other = partner_row[...], other_row[...]
    last = jnp.where(even, other, partner)
    first = jnp.where(even, partner, other)
    before[:64] = pltpu.roll(last, NE, 1)
    before[64:] = last
    after[:64] = first
    after[64:] = pltpu.roll(first, NE, 1)


def column_kernel(own, one, two, three, columns):
    me = lax.axis_index("lev")
    for k, part in enumerate((own, one, two, three)):
        for p in range(4):
            columns[p, lev_rows(me ^ k), :] = part[p]


def lev_rows(lev):
    return pl.ds(pl.multiple_of(32 * lev, 32), 32)


def physics_kernel(columns, mask, mixing, _rim, *rest):
    backs, change = rest[:4], rest[4]
    me = lax.axis_index("lev")
    mix = mixing[...]
    for p in range(4):
        x = columns[p]
        mixed = lax.dot_general(
            mix,
            x,
            (((1,), (0,)), ((), ())),
            precision=lax.Precision.HIGHEST,
            preferred_element_type=jnp.float32,
        )
        heavy = 0.5 * jnp.tanh(mixed) - 0.25 * x
        plain = -0.3 * x / (1.0 + x * x)
        change[p] = jnp.where(mask[p : p + 1, :] == 1, heavy, plain)
        for k in range(4):
            backs[k][p] = change[p, lev_rows(me ^ k), :]


def side_lanes(lane):
    return (lane % NE == 0) | (lane % NE == NE - 1), (lane == 0) | (lane == 127)


def wanted_places(near, edge_of):
    curve = lax.axis_index("curve")
    row0, row63 = rim_rows()
    device = ((near // 128) * 171) // 512
    lane_of = near - E * device
    row_of, along = lane_of // NE, lane_of % NE
    apart = device ^ curve
    k_z, k_x, k_y, k_c = apart // 32, (apart // 8) % 4, (apart // 2) % 4, apart % 2
    in_merged = jnp.where(
        edge_of % 2 == 1,
        24 * k_y + 12 * k_c + jnp.where(edge_of == 3, 0, 6) + row_of,
        96 + jnp.where(edge_of == 0, 0, NE) + along,
    )
    place = PIECE * k_x + MERGED * k_z + in_merged
    lane = lax.broadcasted_iota(jnp.int32, (1, 128), 1)
    side_lane, at_left = side_lanes(lane)

    def row_place(k, row):
        picked = [
            jnp.where(row // 2 == v, place[k : k + 1, 128 * v : 128 * v + 128], 0) for v in range(3)
        ]
        return picked[0] + picked[1] + picked[2]

    sides = jnp.zeros((1, 128), jnp.int32)
    for v in range(3):
        lanes = slice(128 * v, 128 * v + 128)
        both = jnp.where(at_left, place[3:4, lanes], place[1:2, lanes])
        both = jnp.where(side_lane, both, 0)
        sides = sides + (pltpu.roll(both, 2 * v, 1) if v else both)
    return jnp.concatenate([row_place(0, row0), row_place(2, row63), sides], axis=1)


def change_kernel(stepped, own, one, two, three, out):
    me = lax.axis_index("lev")
    for k, part in enumerate((own, one, two, three)):
        for p in range(4):
            at = 4 * (me ^ k) + p
            out[at] = stepped[at] + part[p]


def edge_kernel(stepped, changed, before, after, *rest):
    pools, (wanted_ref, reversed_edge, out, held, sems) = rest[:4], rest[4:]
    row0, row63 = rim_rows()
    turned = reversed_edge[...] == 1
    wanted = wanted_ref[...]
    lane = lax.broadcasted_iota(jnp.int32, (1, 128), 1)
    half = lane // NE
    side_lane, at_left = side_lanes(lane)
    found = None
    for k, pool in enumerate(pools):
        at = lax.broadcasted_iota(jnp.int32, (PIECE, 3 * 128), 0) + PIECE * k
        part = exact_dot((at == wanted).astype(jnp.bfloat16), pool[...], TN)
        found = part if found is None else found + part
    found0, found2, found_side = found[:, :128], found[:, 128:256], found[:, 256:]

    backwards = 127 - lax.broadcasted_iota(jnp.int32, (128, 128), 1)

    def flip(values):
        return jnp.take_along_axis(values, backwards, axis=1)

    def oriented(values, turn):
        four = [values[32 * t : 32 * t + 32] for t in range(4)]
        return [jnp.where(turn, four[3 - t], four[t]) for t in range(4)]

    point = [
        [0, 1, 2, 3],
        [3, 7, 11, 15],
        [12, 13, 14, 15],
        [0, 4, 8, 12],
    ]

    def edge(k, v):
        return jnp.concatenate(
            [stepped[p, :, 128 * v : 128 * v + 128] for p in point[k]], axis=0
        )

    flipped0 = [flip(edge(0, v)) for v in range(3)] + [flip(after[...])]
    flipped2 = [flip(before[...])] + [flip(edge(2, v)) for v in range(3)]
    lower = half == 0
    copies = []
    for v in range(3):
        lanes = slice(128 * v, 128 * v + 128)
        row = 2 * v + half
        own = [edge(k, v) for k in range(4)]
        back = pltpu.roll(found_side, (128 - 2 * v) % 128, 1) if v else found_side
        to_next = [pltpu.roll(own[k], 127, 1) for k in (1, 3)]
        to_last = [pltpu.roll(own[k], 1, 1) for k in (1, 3)]
        across = [
            jnp.where(lower, flipped2[v], flipped2[v + 1]),
            jnp.where(lower, to_next[1], to_last[1]),
            jnp.where(lower, flipped0[v], flipped0[v + 1]),
            jnp.where(lower, to_last[0], to_next[0]),
        ]
        across[0] = jnp.where(row == row0, found0, across[0])
        across[2] = jnp.where(row == row63, found2, across[2])
        across[3] = jnp.where(at_left, back, across[3])
        across[1] = jnp.where(side_lane & ~at_left, back, across[1])
        total = [changed[p, :, lanes] for p in range(16)]
        for k in range(4):
            theirs = oriented(across[k], turned[k : k + 1, lanes])
            for t in range(4):
                p = point[k][t]
                total[p] = total[p] + 0.5 * (theirs[t] - own[k][32 * t : 32 * t + 32])
        for p in range(16):
            held[v, pl.ds(p, 32, stride=16), :] = total[p]
        copies.append(
            pltpu.make_async_copy(held.at[v], out.at[:, pl.ds(128 * v, 128)], sems.at[v])
        )
        copies[-1].start()
    for copy in copies:
        copy.wait()


def on_device(state, wind_x, wind_y, neighbor, neighbor_edge, reversed_edge, branch_mask, mixing):
    flat = state.reshape(512, E)
    part = f32((4, 32, E))
    flat_block, part_block = lane_blocks(512), lane_blocks(4, 32)

    def swap(array, axis, bits):
        devices = lax.axis_size(axis)
        return lax.ppermute(array, axis, [(i, i ^ bits) for i in range(devices)])

    sends = lane_call(split_kernel, (part,) * 4, [flat_block], (part_block,) * 4)(flat)
    cells = [swap(sends[k], "lev", k) for k in (1, 2, 3)]
    stepped, contrib, to_partner, to_other, wanted = lane_call(
        step_kernel,
        (
            f32((16, 32, E)),
            f32((CONTRIB, 128)),
            f32((64, 128)),
            f32((64, 128)),
            jax.ShapeDtypeStruct((1, E), jnp.int32),
        ),
        [flat_block] * 3 + [whole(4, 32, E), whole(4, E), whole(4, E)],
        (whole(16, 32, E), whole(CONTRIB, 128), whole(64, 128), whole(64, 128), whole(1, E)),
    )(
        flat,
        wind_x.reshape(512, E),
        wind_y.reshape(512, E),
        sends[0],
        neighbor,
        neighbor_edge,
    )
    inner = [(i, i + 1) for i in range(1, 62, 2) if i != 31]
    other_row = lax.ppermute(to_other, "curve", inner + [(j, i) for i, j in inner])
    partner_row = swap(to_partner, "curve", 1)
    paired = call(pair_kernel, f32((PAIRED, 128)), 3)(
        contrib, swap(contrib, "curve", 1), partner_row
    )
    along_y = [swap(paired, "curve", k << 1) for k in (1, 2, 3)]
    merged, done = call(merge_kernel, (f32((MERGED, 128)), f32((8, 128))), 4)(paired, *along_y)
    long = pl.CostEstimate(flops=10**11, bytes_accessed=10**8, transcendentals=0)
    columns = call(column_kernel, f32((4, 128, E)), 4, cost=long)(sends[0], *cells)
    backs = call(
        physics_kernel, (part,) * 4, 4, [pltpu.VMEM((4, 128, E), jnp.float32)]
    )(columns, branch_mask, mixing, done)
    changes = [swap(backs[k], "lev", k) for k in (1, 2, 3)]
    piece, before, after = call(
        join_kernel, (f32((2 * MERGED, 128)), f32((128, 128)), f32((128, 128))), 4, cost=long
    )(merged, swap(merged, "curve", 32), partner_row, other_row)
    along_x = [swap(piece, "curve", k << 3) for k in (1, 2, 3)]
    changed = call(change_kernel, f32((16, 32, E)), 5, cost=long)(stepped, backs[0], *changes)
    out = call(
        edge_kernel,
        f32((512, E)),
        10,
        [pltpu.VMEM((3, 512, 128), jnp.float32), pltpu.SemaphoreType.DMA((3,))],
        out_spec=pl.BlockSpec(memory_space=pl.ANY),
    )(stepped, changed, before, after, piece, *along_x, wanted, reversed_edge)
    return out.reshape(32, 16, E)


def solution(mesh):
    in_specs = (
        P("lev", None, "curve"),
        P("lev", None, "curve"),
        P("lev", None, "curve"),
        P(None, "curve"),
        P(None, "curve"),
        P(None, "curve"),
        P("lev", "curve"),
        P(),
    )
    out_specs = P("lev", None, "curve")
    return jax.shard_map(
        on_device, mesh=mesh, in_specs=in_specs, out_specs=out_specs, check_vma=False
    )
```

```python
import functools
import math

import jax
import jax.numpy as jnp
import numpy as np
from jax import lax
from jax.experimental import pallas as pl
from jax.experimental.pallas import tpu as pltpu
from jax.sharding import PartitionSpec as P

NE = 64
ROWS = 6
E = ROWS * NE
CONTRIB = 144
PAIRED = 152
MERGED = 224
PIECE = 2 * MERGED
VMEM = pl.BlockSpec(memory_space=pltpu.VMEM)
ANY = pl.BlockSpec(memory_space=pl.ANY)
LIMIT = 24 * 1024 * 1024
NT = (((1,), (1,)), ((), ()))
TN = (((0,), (0,)), ((), ()))


def derivative_table():
    nodes = np.array([-1.0, -1.0 / math.sqrt(5.0), 1.0 / math.sqrt(5.0), 1.0])
    weights = np.array(
        [1.0 / np.prod([nodes[j] - nodes[m] for m in range(4) if m != j]) for j in range(4)]
    )
    table = np.zeros((4, 4))
    for i in range(4):
        for j in range(4):
            if i == j:
                table[i, j] = sum((1.0 / (nodes[i] - nodes[m]) for m in range(4) if m != i))
            else:
                table[i, j] = weights[j] / weights[i] / (nodes[i] - nodes[j])
    table[1, 1] = table[2, 2] = 0.0
    return table


DERIV = derivative_table()


def f32(shape):
    return jax.ShapeDtypeStruct(shape, jnp.float32)


def call(kernel, out_shape, n_in, scratch=(), out_spec=VMEM, cost=None):
    return pl.pallas_call(
        kernel,
        out_shape=out_shape,
        in_specs=[VMEM] * n_in,
        out_specs=jax.tree.map(lambda _: out_spec, out_shape),
        scratch_shapes=list(scratch),
        compiler_params=pltpu.CompilerParams(vmem_limit_bytes=LIMIT),
        cost_estimate=cost,
    )


def lane_blocks(*leading):
    return pl.BlockSpec((*leading, 128), lambda c: (0,) * len(leading) + (c,))


def whole(*shape):
    return pl.BlockSpec(shape, lambda c: (0,) * len(shape))


def lane_call(kernel, out_shape, in_specs, out_specs):
    return pl.pallas_call(
        kernel,
        grid=(3,),
        out_shape=out_shape,
        in_specs=in_specs,
        out_specs=out_specs,
        compiler_params=pltpu.CompilerParams(vmem_limit_bytes=LIMIT),
    )


def split_kernel(state, *sends):
    me = lax.axis_index("lev")
    for k in range(4):
        first = 4 * (me ^ k)
        for p in range(4):
            sends[k][p] = state[pl.ds(first + p, 32, stride=16), :]


def rim_rows():
    start = lax.axis_index("curve") * ROWS
    return (NE - lax.rem(start, NE)) % NE, NE - 1 - lax.rem(start, NE)


def exact_dot(selector, values, dims):
    high = values.astype(jnp.bfloat16)
    rest = values - high.astype(jnp.float32)
    middle = rest.astype(jnp.bfloat16)
    low = (rest - middle.astype(jnp.float32)).astype(jnp.bfloat16)
    out = None
    for part in (low, middle, high):
        args = (selector, part) if dims == NT else (part, selector)
        term = lax.dot_general(*args, dims, preferred_element_type=jnp.float32)
        out = term if out is None else out + term
    return out


def step_kernel(
    state,
    wind_x,
    wind_y,
    _sent,
    stepped,
    contrib,
    to_partner,
    to_other,
):
    step = pl.program_id(0)
    lanes = pl.ds(pl.multiple_of(128 * step, 128), 128)
    for tile in range(4):
        at = [pl.ds(128 * tile + p, 8, stride=16) for p in range(16)]
        x = [state[at[p], :] for p in range(16)]
        for a in range(4):
            for b in range(4):
                p = 4 * a + b
                dxi = sum(float(DERIV[a, i]) * x[4 * i + b] for i in range(4) if DERIV[a, i])
                deta = sum(float(DERIV[b, j]) * x[4 * a + j] for j in range(4) if DERIV[b, j])
                moved = wind_x[at[p], :] * dxi + wind_y[at[p], :] * deta
                stepped[p, 8 * tile : 8 * tile + 8, lanes] = x[p] - 0.05 * moved

    @pl.when(step == 2)
    def _():
        take_edges(stepped, contrib, to_partner, to_other)


def take_edges(stepped, contrib, to_partner, to_other):
    edge = [
        stepped[0:4].reshape(128, E),
        jnp.concatenate([stepped[4 * t + 3] for t in range(4)], axis=0),
        stepped[12:16].reshape(128, E),
        jnp.concatenate([stepped[4 * t] for t in range(4)], axis=0),
    ]
    last, first = edge[2][:, 256:], edge[0][:, :128]
    low = lax.broadcasted_iota(jnp.int32, (64, 128), 1) < NE
    last = jnp.where(low, pltpu.roll(last[:64], NE, 1), last[64:])
    first = jnp.where(low, first[:64], pltpu.roll(first[64:], NE, 1))
    even = lax.axis_index("curve") % 2 == 0
    to_partner[...] = jnp.where(even, last, first)
    to_other[...] = jnp.where(even, first, last)
    row0, row63 = rim_rows()
    r = lax.broadcasted_iota(jnp.int32, (8, E), 0)
    lane = lax.broadcasted_iota(jnp.int32, (8, E), 1)
    odd = r % 2
    left = ((lane == NE * r + (NE - 1) * odd) & (r < ROWS)).astype(jnp.bfloat16)
    right = ((lane == NE * r + (NE - 1) * (1 - odd)) & (r < ROWS)).astype(jnp.bfloat16)
    contrib[0:6] = exact_dot(left, edge[3], NT)[0:6]
    contrib[6:12] = exact_dot(right, edge[1], NT)[0:6]
    r = lax.broadcasted_iota(jnp.int32, (NE, E), 0)
    lane = lax.broadcasted_iota(jnp.int32, (NE, E), 1)
    contrib[12:76] = exact_dot((lane == NE * row0 + r).astype(jnp.bfloat16), edge[0], NT)
    contrib[76:140] = exact_dot((lane == NE * row63 + r).astype(jnp.bfloat16), edge[2], NT)
    contrib[140:CONTRIB] = jnp.zeros((CONTRIB - 140, 128), jnp.float32)


def pair_kernel(a, b, _row, _one, out):
    out[0:12] = a[0:12]
    out[12:24] = b[0:12]
    out[24:152] = a[12:140] + b[12:140]


def merge_kernel(a, b, c, d, near, edge_of, turns, mask, mixing, *outs):
    out, wanted, turns_out, mask_out, mixing_out = outs
    wanted[...] = wanted_places(near[...], edge_of[...])
    turns_out[...] = turns[...]
    mask_out[...] = mask[...]
    mixing_out[...] = mixing[...]
    for k, part in enumerate((a, b, c, d)):
        out[24 * k : 24 * k + 24] = part[0:24]
    out[96:224] = (a[24:152] + b[24:152]) + (c[24:152] + d[24:152])


def join_kernel(mine, theirs, partner_row, other_row, out, both, before, after):
    out[:MERGED] = mine[...]
    out[MERGED:] = theirs[...]
    for k in range(2):
        both[k, :MERGED] = mine[...]
        both[k, MERGED:] = theirs[...]
    even = lax.axis_index("curve") % 2 == 0
    partner, other = partner_row[...], other_row[...]
    last = jnp.where(even, other, partner)
    first = jnp.where(even, partner, other)
    before[:64] = pltpu.roll(last, NE, 1)
    before[64:] = last
    after[:64] = first
    after[64:] = pltpu.roll(first, NE, 1)


def column_kernel(own, one, two, three, columns):
    me = lax.axis_index("lev")
    for k, part in enumerate((own, one, two, three)):
        for p in range(4):
            columns[p, lev_rows(me ^ k), :] = part[p]


def lev_rows(lev):
    return pl.ds(pl.multiple_of(32 * lev, 32), 32)


def physics_kernel(columns, mask, mixing, *rest):
    backs, change = rest[:4], rest[4]
    me = lax.axis_index("lev")
    mix = mixing[...]
    for p in range(4):
        x = columns[p]
        mixed = lax.dot_general(
            mix,
            x,
            (((1,), (0,)), ((), ())),
            precision=lax.Precision.HIGHEST,
            preferred_element_type=jnp.float32,
        )
        heavy = 0.5 * jnp.tanh(mixed) - 0.25 * x
        plain = -0.3 * x / (1.0 + x * x)
        change[p] = jnp.where(mask[p : p + 1, :] == 1, heavy, plain)
        for k in range(4):
            backs[k][p] = change[p, lev_rows(me ^ k), :]


def side_lanes(lane):
    return (lane % NE == 0) | (lane % NE == NE - 1), (lane == 0) | (lane == 127)


def wanted_places(near, edge_of):
    curve = lax.axis_index("curve")
    row0, row63 = rim_rows()
    device = ((near // 128) * 171) // 512
    lane_of = near - E * device
    row_of, along = lane_of // NE, lane_of % NE
    apart = device ^ curve
    k_z, k_x, k_y, k_c = apart // 32, (apart // 8) % 4, (apart // 2) % 4, apart % 2
    in_merged = jnp.where(
        edge_of % 2 == 1,
        24 * k_y + 12 * k_c + jnp.where(edge_of == 3, 0, 6) + row_of,
        96 + jnp.where(edge_of == 0, 0, NE) + along,
    )
    place = PIECE * k_x + MERGED * k_z + in_merged
    lane = lax.broadcasted_iota(jnp.int32, (1, 128), 1)
    side_lane, at_left = side_lanes(lane)

    def row_place(k, row):
        picked = [
            jnp.where(row // 2 == v, place[k : k + 1, 128 * v : 128 * v + 128], 0) for v in range(3)
        ]
        return picked[0] + picked[1] + picked[2]

    sides = jnp.zeros((1, 128), jnp.int32)
    for v in range(3):
        lanes = slice(128 * v, 128 * v + 128)
        both = jnp.where(at_left, place[3:4, lanes], place[1:2, lanes])
        both = jnp.where(side_lane, both, 0)
        sides = sides + (pltpu.roll(both, 2 * v, 1) if v else both)
    return jnp.concatenate([row_place(0, row0), row_place(2, row63), sides], axis=1)


def change_kernel(base, own, one, two, three, out):
    me = lax.axis_index("lev")
    for k, part in enumerate((own, one, two, three)):
        for p in range(4):
            at = 4 * (me ^ k) + p
            out[at] = base[at] + part[p]


POINT = [[0, 1, 2, 3], [3, 7, 11, 15], [12, 13, 14, 15], [0, 4, 8, 12]]


def edge_of_tile(stepped, k, v):
    return jnp.concatenate([stepped[p, :, 128 * v : 128 * v + 128] for p in POINT[k]], axis=0)


def oriented(values, turn):
    four = [values[32 * t : 32 * t + 32] for t in range(4)]
    return [jnp.where(turn, four[3 - t], four[t]) for t in range(4)]


def rim_masks(v):
    row0, row63 = rim_rows()
    lane = lax.broadcasted_iota(jnp.int32, (1, 128), 1)
    row = 2 * v + lane // NE
    side_lane, at_left = side_lanes(lane)
    return [row == row0, side_lane & ~at_left, row == row63, at_left]


def near_kernel(stepped, before, after, turns, base):
    turned = turns[...] == 1
    backwards = 127 - lax.broadcasted_iota(jnp.int32, (128, 128), 1)

    def flip(values):
        return jnp.take_along_axis(values, backwards, axis=1)

    lower = lax.broadcasted_iota(jnp.int32, (1, 128), 1) < NE
    flipped0 = [flip(edge_of_tile(stepped, 0, v)) for v in range(3)] + [flip(after[...])]
    flipped2 = [flip(before[...])] + [flip(edge_of_tile(stepped, 2, v)) for v in range(3)]
    for v in range(3):
        lanes = slice(128 * v, 128 * v + 128)
        own = [edge_of_tile(stepped, k, v) for k in range(4)]
        to_next = [pltpu.roll(own[k], 127, 1) for k in (1, 3)]
        to_last = [pltpu.roll(own[k], 1, 1) for k in (1, 3)]
        across = [
            jnp.where(lower, flipped2[v], flipped2[v + 1]),
            jnp.where(lower, to_next[1], to_last[1]),
            jnp.where(lower, flipped0[v], flipped0[v + 1]),
            jnp.where(lower, to_last[0], to_next[0]),
        ]
        total = [stepped[p, :, lanes] for p in range(16)]
        far = rim_masks(v)
        for k in range(4):
            theirs = oriented(across[k], turned[k : k + 1, lanes])
            for t in range(4):
                p = POINT[k][t]
                term = 0.5 * (theirs[t] - own[k][32 * t : 32 * t + 32])
                total[p] = total[p] + jnp.where(far[k], 0.0, term)
        for p in range(16):
            base[p, :, lanes] = total[p]


def edge_kernel(stepped, changed, own, one, both, three, wanted, turns, out, held, sems):
    other = 1 - (lax.axis_index("curve") // 16) % 2
    pools = own, one, both.at[other], three
    turned = turns[...] == 1
    found = None
    for k, pool in enumerate(pools):
        at = lax.broadcasted_iota(jnp.int32, (PIECE, 3 * 128), 0) + PIECE * k
        part = exact_dot((at == wanted[...]).astype(jnp.bfloat16), pool[...], TN)
        found = part if found is None else found + part
    found0, found2, found_side = found[:, :128], found[:, 128:256], found[:, 256:]
    copies = []
    for v in range(3):
        lanes = slice(128 * v, 128 * v + 128)
        back = pltpu.roll(found_side, (128 - 2 * v) % 128, 1) if v else found_side
        total = [changed[p, :, lanes] for p in range(16)]
        far = rim_masks(v)
        for k, across in enumerate((found0, back, found2, back)):
            own = edge_of_tile(stepped, k, v)
            theirs = oriented(across, turned[k : k + 1, lanes])
            for t in range(4):
                p = POINT[k][t]
                term = 0.5 * (theirs[t] - own[32 * t : 32 * t + 32])
                total[p] = total[p] + jnp.where(far[k], term, 0.0)
        for p in range(16):
            held[v, pl.ds(p, 32, stride=16), :] = total[p]
        copies.append(
            pltpu.make_async_copy(held.at[v], out.at[:, pl.ds(128 * v, 128)], sems.at[v])
        )
        copies[-1].start()
    for copy in copies:
        copy.wait()


def on_device(state, wind_x, wind_y, neighbor, neighbor_edge, reversed_edge, branch_mask, mixing):
    flat = state.reshape(512, E)
    part = f32((4, 32, E))
    flat_block, part_block = lane_blocks(512), lane_blocks(4, 32)

    def swap(array, axis, bits):
        devices = lax.axis_size(axis)
        return lax.ppermute(array, axis, [(i, i ^ bits) for i in range(devices)])

    sends = lane_call(split_kernel, (part,) * 4, [flat_block], (part_block,) * 4)(flat)
    cells = [swap(sends[k], "lev", k) for k in (1, 2, 3)]
    stepped, contrib, to_partner, to_other = lane_call(
        step_kernel,
        (
            f32((16, 32, E)),
            f32((CONTRIB, 128)),
            f32((64, 128)),
            f32((64, 128)),
        ),
        [flat_block] * 3 + [whole(4, 32, E)],
        (whole(16, 32, E), whole(CONTRIB, 128), whole(64, 128), whole(64, 128)),
    )(
        flat,
        wind_x.reshape(512, E),
        wind_y.reshape(512, E),
        sends[0],
    )
    inner = [(i, i + 1) for i in range(1, 62, 2) if i != 31]
    other_row = lax.ppermute(to_other, "curve", inner + [(j, i) for i, j in inner])
    partner_row = swap(to_partner, "curve", 1)
    paired = call(pair_kernel, f32((PAIRED, 128)), 4)(
        contrib, swap(contrib, "curve", 1), partner_row, cells[0]
    )
    along_y = [swap(paired, "curve", k << 1) for k in (1, 2, 3)]
    table = jax.ShapeDtypeStruct((4, E), jnp.int32)
    merged, wanted, turns, mask, mix = call(
        merge_kernel,
        (
            f32((MERGED, 128)),
            jax.ShapeDtypeStruct((1, E), jnp.int32),
            table,
            table,
            f32((128, 128)),
        ),
        9,
    )(paired, *along_y, neighbor, neighbor_edge, reversed_edge, branch_mask, mixing)
    long = pl.CostEstimate(flops=10**11, bytes_accessed=10**8, transcendentals=0)
    columns = call(column_kernel, f32((4, 128, E)), 4, cost=long)(sends[0], *cells)
    backs = call(
        physics_kernel, (part,) * 4, 3, [pltpu.VMEM((4, 128, E), jnp.float32)]
    )(columns, mask, mix)
    changes = [swap(backs[k], "lev", k) for k in (1, 2, 3)]
    piece, twice, before, after = call(
        join_kernel,
        (f32((PIECE, 128)), f32((2, PIECE, 128)), f32((128, 128)), f32((128, 128))),
        4,
        cost=long,
    )(merged, swap(merged, "curve", 32), partner_row, other_row)
    along_x = [swap(piece, "curve", k << 3) for k in (1, 3)]
    groups = [[i, i ^ 16] for i in range(64) if not i & 16]
    across_x = lax.all_to_all(twice, "curve", 0, 0, axis_index_groups=groups, tiled=True)
    base = call(near_kernel, f32((16, 32, E)), 4)(stepped, before, after, turns)
    changed = call(change_kernel, f32((16, 32, E)), 5, cost=long)(base, backs[0], *changes)
    out = call(
        edge_kernel,
        f32((512, E)),
        8,
        [pltpu.VMEM((3, 512, 128), jnp.float32), pltpu.SemaphoreType.DMA((3,))],
        out_spec=pl.BlockSpec(memory_space=pl.ANY),
    )(stepped, changed, piece, along_x[0], across_x, along_x[1], wanted, turns)
    return out.reshape(32, 16, E)


def solution(mesh):
    in_specs = (
        P("lev", None, "curve"),
        P("lev", None, "curve"),
        P("lev", None, "curve"),
        P(None, "curve"),
        P(None, "curve"),
        P(None, "curve"),
        P("lev", "curve"),
        P(),
    )
    out_specs = P("lev", None, "curve")
    return jax.shard_map(
        on_device, mesh=mesh, in_specs=in_specs, out_specs=out_specs, check_vma=False
    )
```

```python
import functools
import math

import jax
import jax.numpy as jnp
import numpy as np
from jax import lax
from jax.experimental import pallas as pl
from jax.experimental.pallas import tpu as pltpu
from jax.sharding import PartitionSpec as P

NE = 64
ROWS = 6
E = ROWS * NE
CONTRIB = 144
PAIRED = 152
MERGED = 224
HALF = 4 * MERGED
VMEM = pl.BlockSpec(memory_space=pltpu.VMEM)
ANY = pl.BlockSpec(memory_space=pl.ANY)
LIMIT = 24 * 1024 * 1024
NT = (((1,), (1,)), ((), ()))
TN = (((0,), (0,)), ((), ()))


def derivative_table():
    nodes = np.array([-1.0, -1.0 / math.sqrt(5.0), 1.0 / math.sqrt(5.0), 1.0])
    weights = np.array(
        [1.0 / np.prod([nodes[j] - nodes[m] for m in range(4) if m != j]) for j in range(4)]
    )
    table = np.zeros((4, 4))
    for i in range(4):
        for j in range(4):
            if i == j:
                table[i, j] = sum((1.0 / (nodes[i] - nodes[m]) for m in range(4) if m != i))
            else:
                table[i, j] = weights[j] / weights[i] / (nodes[i] - nodes[j])
    table[1, 1] = table[2, 2] = 0.0
    return table


DERIV = derivative_table()


def f32(shape):
    return jax.ShapeDtypeStruct(shape, jnp.float32)


def call(kernel, out_shape, n_in, scratch=(), out_spec=VMEM, cost=None):
    return pl.pallas_call(
        kernel,
        out_shape=out_shape,
        in_specs=[VMEM] * n_in,
        out_specs=jax.tree.map(lambda _: out_spec, out_shape),
        scratch_shapes=list(scratch),
        compiler_params=pltpu.CompilerParams(vmem_limit_bytes=LIMIT),
        cost_estimate=cost,
    )


def lane_blocks(*leading):
    return pl.BlockSpec((*leading, 128), lambda c: (0,) * len(leading) + (c,))


def whole(*shape):
    return pl.BlockSpec(shape, lambda c: (0,) * len(shape))


def lane_call(kernel, out_shape, in_specs, out_specs):
    return pl.pallas_call(
        kernel,
        grid=(3,),
        out_shape=out_shape,
        in_specs=in_specs,
        out_specs=out_specs,
        compiler_params=pltpu.CompilerParams(vmem_limit_bytes=LIMIT),
    )


def split_kernel(state, *sends):
    me = lax.axis_index("lev")
    for k in range(4):
        first = 4 * (me ^ k)
        for p in range(4):
            sends[k][p] = state[pl.ds(first + p, 32, stride=16), :]


def rim_rows():
    start = lax.axis_index("curve") * ROWS
    return (NE - lax.rem(start, NE)) % NE, NE - 1 - lax.rem(start, NE)


def exact_dot(selector, values, dims):
    high = values.astype(jnp.bfloat16)
    rest = values - high.astype(jnp.float32)
    middle = rest.astype(jnp.bfloat16)
    low = (rest - middle.astype(jnp.float32)).astype(jnp.bfloat16)
    out = None
    for part in (low, middle, high):
        args = (selector, part) if dims == NT else (part, selector)
        term = lax.dot_general(*args, dims, preferred_element_type=jnp.float32)
        out = term if out is None else out + term
    return out


def step_kernel(
    state,
    wind_x,
    wind_y,
    _sent,
    stepped,
    contrib,
    to_partner,
    to_other,
):
    step = pl.program_id(0)
    lanes = pl.ds(pl.multiple_of(128 * step, 128), 128)
    for tile in range(4):
        at = [pl.ds(128 * tile + p, 8, stride=16) for p in range(16)]
        x = [state[at[p], :] for p in range(16)]
        for a in range(4):
            for b in range(4):
                p = 4 * a + b
                dxi = sum(float(DERIV[a, i]) * x[4 * i + b] for i in range(4) if DERIV[a, i])
                deta = sum(float(DERIV[b, j]) * x[4 * a + j] for j in range(4) if DERIV[b, j])
                moved = wind_x[at[p], :] * dxi + wind_y[at[p], :] * deta
                stepped[p, 8 * tile : 8 * tile + 8, lanes] = x[p] - 0.05 * moved

    @pl.when(step == 2)
    def _():
        take_edges(stepped, contrib, to_partner, to_other)


def take_edges(stepped, contrib, to_partner, to_other):
    edge = [
        stepped[0:4].reshape(128, E),
        jnp.concatenate([stepped[4 * t + 3] for t in range(4)], axis=0),
        stepped[12:16].reshape(128, E),
        jnp.concatenate([stepped[4 * t] for t in range(4)], axis=0),
    ]
    last, first = edge[2][:, 256:], edge[0][:, :128]
    low = lax.broadcasted_iota(jnp.int32, (64, 128), 1) < NE
    last = jnp.where(low, pltpu.roll(last[:64], NE, 1), last[64:])
    first = jnp.where(low, first[:64], pltpu.roll(first[64:], NE, 1))
    even = lax.axis_index("curve") % 2 == 0
    to_partner[...] = jnp.where(even, last, first)
    to_other[...] = jnp.where(even, first, last)
    row0, row63 = rim_rows()
    r = lax.broadcasted_iota(jnp.int32, (8, E), 0)
    lane = lax.broadcasted_iota(jnp.int32, (8, E), 1)
    odd = r % 2
    left = ((lane == NE * r + (NE - 1) * odd) & (r < ROWS)).astype(jnp.bfloat16)
    right = ((lane == NE * r + (NE - 1) * (1 - odd)) & (r < ROWS)).astype(jnp.bfloat16)
    contrib[0:6] = exact_dot(left, edge[3], NT)[0:6]
    contrib[6:12] = exact_dot(right, edge[1], NT)[0:6]
    r = lax.broadcasted_iota(jnp.int32, (NE, E), 0)
    lane = lax.broadcasted_iota(jnp.int32, (NE, E), 1)
    contrib[12:76] = exact_dot((lane == NE * row0 + r).astype(jnp.bfloat16), edge[0], NT)
    contrib[76:140] = exact_dot((lane == NE * row63 + r).astype(jnp.bfloat16), edge[2], NT)
    contrib[140:CONTRIB] = jnp.zeros((CONTRIB - 140, 128), jnp.float32)


def pair_kernel(a, b, _row, _one, out):
    even = lax.axis_index("curve") % 2 == 0
    out[0:12] = jnp.where(even, a[0:12], b[0:12])
    out[12:24] = jnp.where(even, b[0:12], a[0:12])
    out[24:152] = a[12:140] + b[12:140]


def merge_kernel(a, b, c, d, near, edge_of, turns, mask, mixing, *outs):
    out, wanted, turns_out, mask_out, mixing_out = outs
    wanted[...] = wanted_places(near[...], edge_of[...])
    turns_out[...] = turns[...]
    mask_out[...] = mask[...]
    mixing_out[...] = mixing[...]
    for k, part in enumerate((a, b, c, d)):
        out[24 * k : 24 * k + 24] = part[0:24]
    out[96:224] = (a[24:152] + b[24:152]) + (c[24:152] + d[24:152])


def join_kernel(mine, theirs, partner_row, other_row, out, both, before, after):
    half = jnp.where(lax.axis_index("curve") % 2 == 0, mine[...], theirs[...])
    out[...] = half
    for k in range(2):
        both[k] = half
    even = lax.axis_index("curve") % 2 == 0
    partner, other = partner_row[...], other_row[...]
    last = jnp.where(even, other, partner)
    first = jnp.where(even, partner, other)
    before[:64] = pltpu.roll(last, NE, 1)
    before[64:] = last
    after[:64] = first
    after[64:] = pltpu.roll(first, NE, 1)


def column_kernel(own, one, two, three, columns):
    me = lax.axis_index("lev")
    for k, part in enumerate((own, one, two, three)):
        for p in range(4):
            columns[p, lev_rows(me ^ k), :] = part[p]


def lev_rows(lev):
    return pl.ds(pl.multiple_of(32 * lev, 32), 32)


def physics_kernel(columns, mask, mixing, _wanted, *rest):
    backs, change = rest[:4], rest[4]
    me = lax.axis_index("lev")
    mix = mixing[...]
    for p in range(4):
        x = columns[p]
        mixed = lax.dot_general(
            mix,
            x,
            (((1,), (0,)), ((), ())),
            precision=lax.Precision.HIGHEST,
            preferred_element_type=jnp.float32,
        )
        heavy = 0.5 * jnp.tanh(mixed) - 0.25 * x
        plain = -0.3 * x / (1.0 + x * x)
        change[p] = jnp.where(mask[p : p + 1, :] == 1, heavy, plain)
        for k in range(4):
            backs[k][p] = change[p, lev_rows(me ^ k), :]


def side_lanes(lane):
    return (lane % NE == 0) | (lane % NE == NE - 1), (lane == 0) | (lane == 127)


def wanted_places(near, edge_of):
    curve = lax.axis_index("curve")
    row0, row63 = rim_rows()
    device = ((near // 128) * 171) // 512
    lane_of = near - E * device
    row_of, along = lane_of // NE, lane_of % NE
    apart = device ^ curve
    k_x, k_y = (apart // 8) % 4, (apart // 2) % 4
    in_merged = jnp.where(
        edge_of % 2 == 1,
        24 * k_y + 12 * (device % 2) + jnp.where(edge_of == 3, 0, 6) + row_of,
        96 + jnp.where(edge_of == 0, 0, NE) + along,
    )
    place = HALF * (apart // 32) + MERGED * k_x + in_merged
    lane = lax.broadcasted_iota(jnp.int32, (1, 128), 1)
    side_lane, at_left = side_lanes(lane)

    def row_place(k, row):
        picked = [
            jnp.where(row // 2 == v, place[k : k + 1, 128 * v : 128 * v + 128], 0) for v in range(3)
        ]
        return picked[0] + picked[1] + picked[2]

    sides = jnp.zeros((1, 128), jnp.int32)
    for v in range(3):
        lanes = slice(128 * v, 128 * v + 128)
        both = jnp.where(at_left, place[3:4, lanes], place[1:2, lanes])
        both = jnp.where(side_lane, both, 0)
        sides = sides + (pltpu.roll(both, 2 * v, 1) if v else both)
    return jnp.concatenate([row_place(0, row0), row_place(2, row63), sides], axis=1)


def change_kernel(base, own, one, two, three, out):
    me = lax.axis_index("lev")
    for k, part in enumerate((own, one, two, three)):
        for p in range(4):
            at = 4 * (me ^ k) + p
            out[at] = base[at] + part[p]


POINT = [[0, 1, 2, 3], [3, 7, 11, 15], [12, 13, 14, 15], [0, 4, 8, 12]]


def edge_of_tile(stepped, k, v):
    return jnp.concatenate([stepped[p, :, 128 * v : 128 * v + 128] for p in POINT[k]], axis=0)


def oriented(values, turn):
    four = [values[32 * t : 32 * t + 32] for t in range(4)]
    return [jnp.where(turn, four[3 - t], four[t]) for t in range(4)]


def rim_masks(v):
    row0, row63 = rim_rows()
    lane = lax.broadcasted_iota(jnp.int32, (1, 128), 1)
    row = 2 * v + lane // NE
    side_lane, at_left = side_lanes(lane)
    return [row == row0, side_lane & ~at_left, row == row63, at_left]


def near_kernel(stepped, before, after, turns, base):
    turned = turns[...] == 1
    backwards = 127 - lax.broadcasted_iota(jnp.int32, (128, 128), 1)

    def flip(values):
        return jnp.take_along_axis(values, backwards, axis=1)

    lower = lax.broadcasted_iota(jnp.int32, (1, 128), 1) < NE
    flipped0 = [flip(edge_of_tile(stepped, 0, v)) for v in range(3)] + [flip(after[...])]
    flipped2 = [flip(before[...])] + [flip(edge_of_tile(stepped, 2, v)) for v in range(3)]
    for v in range(3):
        lanes = slice(128 * v, 128 * v + 128)
        own = [edge_of_tile(stepped, k, v) for k in range(4)]
        to_next = [pltpu.roll(own[k], 127, 1) for k in (1, 3)]
        to_last = [pltpu.roll(own[k], 1, 1) for k in (1, 3)]
        across = [
            jnp.where(lower, flipped2[v], flipped2[v + 1]),
            jnp.where(lower, to_next[1], to_last[1]),
            jnp.where(lower, flipped0[v], flipped0[v + 1]),
            jnp.where(lower, to_last[0], to_next[0]),
        ]
        total = [stepped[p, :, lanes] for p in range(16)]
        far = rim_masks(v)
        for k in range(4):
            theirs = oriented(across[k], turned[k : k + 1, lanes])
            for t in range(4):
                p = POINT[k][t]
                term = 0.5 * (theirs[t] - own[k][32 * t : 32 * t + 32])
                total[p] = total[p] + jnp.where(far[k], 0.0, term)
        for p in range(16):
            base[p, :, lanes] = total[p]


def pick_kernel(own, one, both, three, wanted, partner_wanted, mine, theirs):
    curve = lax.axis_index("curve")
    pools = own, one, both.at[1 - (curve // 16) % 2], three
    want = jnp.concatenate([wanted[...], partner_wanted[...]], axis=1)
    found = None
    for k, pool in enumerate(pools):
        at = lax.broadcasted_iota(jnp.int32, (MERGED, 2 * E), 0) + (MERGED * k + HALF * (curve % 2))
        part = exact_dot((at == want).astype(jnp.bfloat16), pool[...], TN)
        found = part if found is None else found + part
    mine[...] = found[:, :E]
    theirs[...] = found[:, E:]


def edge_kernel(stepped, changed, mine, theirs, turns, out, held, sems):
    turned = turns[...] == 1
    found = mine[...] + theirs[...]
    found0, found2, found_side = found[:, :128], found[:, 128:256], found[:, 256:]
    copies = []
    for v in range(3):
        lanes = slice(128 * v, 128 * v + 128)
        back = pltpu.roll(found_side, (128 - 2 * v) % 128, 1) if v else found_side
        total = [changed[p, :, lanes] for p in range(16)]
        far = rim_masks(v)
        for k, across in enumerate((found0, back, found2, back)):
            own = edge_of_tile(stepped, k, v)
            theirs = oriented(across, turned[k : k + 1, lanes])
            for t in range(4):
                p = POINT[k][t]
                term = 0.5 * (theirs[t] - own[32 * t : 32 * t + 32])
                total[p] = total[p] + jnp.where(far[k], term, 0.0)
        for p in range(16):
            held[v, pl.ds(p, 32, stride=16), :] = total[p]
        copies.append(
            pltpu.make_async_copy(held.at[v], out.at[:, pl.ds(128 * v, 128)], sems.at[v])
        )
        copies[-1].start()
    for copy in copies:
        copy.wait()


def on_device(state, wind_x, wind_y, neighbor, neighbor_edge, reversed_edge, branch_mask, mixing):
    flat = state.reshape(512, E)
    part = f32((4, 32, E))
    flat_block, part_block = lane_blocks(512), lane_blocks(4, 32)

    def swap(array, axis, bits):
        devices = lax.axis_size(axis)
        return lax.ppermute(array, axis, [(i, i ^ bits) for i in range(devices)])

    sends = lane_call(split_kernel, (part,) * 4, [flat_block], (part_block,) * 4)(flat)
    cells = [swap(sends[k], "lev", k) for k in (1, 2, 3)]
    stepped, contrib, to_partner, to_other = lane_call(
        step_kernel,
        (
            f32((16, 32, E)),
            f32((CONTRIB, 128)),
            f32((64, 128)),
            f32((64, 128)),
        ),
        [flat_block] * 3 + [whole(4, 32, E)],
        (whole(16, 32, E), whole(CONTRIB, 128), whole(64, 128), whole(64, 128)),
    )(
        flat,
        wind_x.reshape(512, E),
        wind_y.reshape(512, E),
        sends[0],
    )
    inner = [(i, i + 1) for i in range(1, 62, 2) if i != 31]
    other_row = lax.ppermute(to_other, "curve", inner + [(j, i) for i, j in inner])
    partner_row = swap(to_partner, "curve", 1)
    paired = call(pair_kernel, f32((PAIRED, 128)), 4)(
        contrib, swap(contrib, "curve", 1), partner_row, cells[0]
    )
    along_y = [swap(paired, "curve", k << 1) for k in (1, 2, 3)]
    table = jax.ShapeDtypeStruct((4, E), jnp.int32)
    merged, wanted, turns, mask, mix = call(
        merge_kernel,
        (
            f32((MERGED, 128)),
            jax.ShapeDtypeStruct((1, E), jnp.int32),
            table,
            table,
            f32((128, 128)),
        ),
        9,
    )(paired, *along_y, neighbor, neighbor_edge, reversed_edge, branch_mask, mixing)
    partner_wanted = swap(wanted, "curve", 1)
    other_half = lax.ppermute(
        merged,
        "curve",
        [(i, i ^ 32) for i in range(1, 64, 2)],
    )
    long = pl.CostEstimate(flops=10**11, bytes_accessed=10**8, transcendentals=0)
    columns = call(column_kernel, f32((4, 128, E)), 4, cost=long)(sends[0], *cells)
    backs = call(
        physics_kernel, (part,) * 4, 4, [pltpu.VMEM((4, 128, E), jnp.float32)]
    )(columns, mask, mix, partner_wanted)
    changes = [swap(backs[k], "lev", k) for k in (1, 2, 3)]
    piece, twice, before, after = call(
        join_kernel,
        (f32((MERGED, 128)), f32((2, MERGED, 128)), f32((128, 128)), f32((128, 128))),
        4,
        cost=long,
    )(merged, other_half, partner_row, other_row)
    along_x = [swap(piece, "curve", k << 3) for k in (1, 3)]
    groups = [[i, i ^ 16] for i in range(64) if not i & 16]
    across_x = lax.all_to_all(twice, "curve", 0, 0, axis_index_groups=groups, tiled=True)
    base = call(near_kernel, f32((16, 32, E)), 4)(stepped, before, after, turns)
    changed = call(change_kernel, f32((16, 32, E)), 5, cost=long)(base, backs[0], *changes)
    mine, theirs = call(pick_kernel, (f32((128, E)), f32((128, E))), 6)(
        piece, along_x[0], across_x, along_x[1], wanted, partner_wanted
    )
    out = call(
        edge_kernel,
        f32((512, E)),
        5,
        [pltpu.VMEM((3, 512, 128), jnp.float32), pltpu.SemaphoreType.DMA((3,))],
        out_spec=pl.BlockSpec(memory_space=pl.ANY),
    )(stepped, changed, mine, swap(theirs, "curve", 1), turns)
    return out.reshape(32, 16, E)


def solution(mesh):
    in_specs = (
        P("lev", None, "curve"),
        P("lev", None, "curve"),
        P("lev", None, "curve"),
        P(None, "curve"),
        P(None, "curve"),
        P(None, "curve"),
        P("lev", "curve"),
        P(),
    )
    out_specs = P("lev", None, "curve")
    return jax.shard_map(
        on_device, mesh=mesh, in_specs=in_specs, out_specs=out_specs, check_vma=False
    )
```

```python
import functools
import math

import jax
import jax.numpy as jnp
import numpy as np
from jax import lax
from jax.experimental import pallas as pl
from jax.experimental.pallas import tpu as pltpu
from jax.sharding import PartitionSpec as P

NE = 64
ROWS = 6
E = ROWS * NE
CONTRIB = 144
PAIRED = 152
MERGED = 224
HALF = 4 * MERGED
VMEM = pl.BlockSpec(memory_space=pltpu.VMEM)
ANY = pl.BlockSpec(memory_space=pl.ANY)
LIMIT = 24 * 1024 * 1024
NT = (((1,), (1,)), ((), ()))
TN = (((0,), (0,)), ((), ()))


def derivative_table():
    nodes = np.array([-1.0, -1.0 / math.sqrt(5.0), 1.0 / math.sqrt(5.0), 1.0])
    weights = np.array(
        [1.0 / np.prod([nodes[j] - nodes[m] for m in range(4) if m != j]) for j in range(4)]
    )
    table = np.zeros((4, 4))
    for i in range(4):
        for j in range(4):
            if i == j:
                table[i, j] = sum((1.0 / (nodes[i] - nodes[m]) for m in range(4) if m != i))
            else:
                table[i, j] = weights[j] / weights[i] / (nodes[i] - nodes[j])
    table[1, 1] = table[2, 2] = 0.0
    return table


DERIV = derivative_table()


def f32(shape):
    return jax.ShapeDtypeStruct(shape, jnp.float32)


def call(kernel, out_shape, n_in, scratch=(), out_spec=VMEM, cost=None):
    return pl.pallas_call(
        kernel,
        out_shape=out_shape,
        in_specs=[VMEM] * n_in,
        out_specs=jax.tree.map(lambda _: out_spec, out_shape),
        scratch_shapes=list(scratch),
        compiler_params=pltpu.CompilerParams(vmem_limit_bytes=LIMIT),
        cost_estimate=cost,
    )


def lane_blocks(*leading):
    return pl.BlockSpec((*leading, 128), lambda c: (0,) * len(leading) + (c,))


def whole(*shape):
    return pl.BlockSpec(shape, lambda c: (0,) * len(shape))


def lane_call(kernel, out_shape, in_specs, out_specs):
    return pl.pallas_call(
        kernel,
        grid=(3,),
        out_shape=out_shape,
        in_specs=in_specs,
        out_specs=out_specs,
        compiler_params=pltpu.CompilerParams(vmem_limit_bytes=LIMIT),
    )


def split_kernel(state, *sends):
    me = lax.axis_index("lev")
    for k in range(4):
        first = 4 * (me ^ k)
        for p in range(4):
            sends[k][p] = state[pl.ds(first + p, 32, stride=16), :]


def rim_rows():
    start = lax.axis_index("curve") * ROWS
    return (NE - lax.rem(start, NE)) % NE, NE - 1 - lax.rem(start, NE)


def exact_dot(selector, values, dims):
    high = values.astype(jnp.bfloat16)
    rest = values - high.astype(jnp.float32)
    middle = rest.astype(jnp.bfloat16)
    low = (rest - middle.astype(jnp.float32)).astype(jnp.bfloat16)
    out = None
    for part in (low, middle, high):
        args = (selector, part) if dims == NT else (part, selector)
        term = lax.dot_general(*args, dims, preferred_element_type=jnp.float32)
        out = term if out is None else out + term
    return out


def step_kernel(
    state,
    wind_x,
    wind_y,
    _sent,
    stepped,
    contrib,
    to_partner,
    to_other,
):
    step = pl.program_id(0)
    lanes = pl.ds(pl.multiple_of(128 * step, 128), 128)
    for tile in range(4):
        at = [pl.ds(128 * tile + p, 8, stride=16) for p in range(16)]
        x = [state[at[p], :] for p in range(16)]
        for a in range(4):
            for b in range(4):
                p = 4 * a + b
                dxi = sum(float(DERIV[a, i]) * x[4 * i + b] for i in range(4) if DERIV[a, i])
                deta = sum(float(DERIV[b, j]) * x[4 * a + j] for j in range(4) if DERIV[b, j])
                moved = wind_x[at[p], :] * dxi + wind_y[at[p], :] * deta
                stepped[p, 8 * tile : 8 * tile + 8, lanes] = x[p] - 0.05 * moved

    @pl.when(step == 2)
    def _():
        take_edges(stepped, contrib, to_partner, to_other)


def take_edges(stepped, contrib, to_partner, to_other):
    edge = [
        stepped[0:4].reshape(128, E),
        jnp.concatenate([stepped[4 * t + 3] for t in range(4)], axis=0),
        stepped[12:16].reshape(128, E),
        jnp.concatenate([stepped[4 * t] for t in range(4)], axis=0),
    ]
    last, first = edge[2][:, 256:], edge[0][:, :128]
    low = lax.broadcasted_iota(jnp.int32, (64, 128), 1) < NE
    last = jnp.where(low, pltpu.roll(last[:64], NE, 1), last[64:])
    first = jnp.where(low, first[:64], pltpu.roll(first[64:], NE, 1))
    even = lax.axis_index("curve") % 2 == 0
    to_partner[...] = jnp.where(even, last, first)
    to_other[...] = jnp.where(even, first, last)
    row0, row63 = rim_rows()
    r = lax.broadcasted_iota(jnp.int32, (8, E), 0)
    lane = lax.broadcasted_iota(jnp.int32, (8, E), 1)
    odd = r % 2
    left = ((lane == NE * r + (NE - 1) * odd) & (r < ROWS)).astype(jnp.bfloat16)
    right = ((lane == NE * r + (NE - 1) * (1 - odd)) & (r < ROWS)).astype(jnp.bfloat16)
    contrib[0:6] = exact_dot(left, edge[3], NT)[0:6]
    contrib[6:12] = exact_dot(right, edge[1], NT)[0:6]
    r = lax.broadcasted_iota(jnp.int32, (NE, E), 0)
    lane = lax.broadcasted_iota(jnp.int32, (NE, E), 1)
    contrib[12:76] = exact_dot((lane == NE * row0 + r).astype(jnp.bfloat16), edge[0], NT)
    contrib[76:140] = exact_dot((lane == NE * row63 + r).astype(jnp.bfloat16), edge[2], NT)
    contrib[140:CONTRIB] = jnp.zeros((CONTRIB - 140, 128), jnp.float32)


def pair_kernel(a, b, _row, _one, out):
    even = lax.axis_index("curve") % 2 == 0
    out[0:12] = jnp.where(even, a[0:12], b[0:12])
    out[12:24] = jnp.where(even, b[0:12], a[0:12])
    out[24:152] = a[12:140] + b[12:140]


def merge_kernel(a, b, c, d, near, edge_of, turns, mask, mixing, *outs):
    out, wanted, turns_out, mask_out, mixing_out = outs
    wanted[...] = wanted_places(near[...], edge_of[...])
    turns_out[...] = turns[...]
    mask_out[...] = mask[...]
    mixing_out[...] = mixing[...]
    for k, part in enumerate((a, b, c, d)):
        out[24 * k : 24 * k + 24] = part[0:24]
    out[96:224] = (a[24:152] + b[24:152]) + (c[24:152] + d[24:152])


def join_kernel(mine, theirs, partner_row, other_row, out, both, before, after):
    half = jnp.where(lax.axis_index("curve") % 2 == 0, mine[...], theirs[...])
    out[...] = half
    for k in range(2):
        both[k] = half
    even = lax.axis_index("curve") % 2 == 0
    partner, other = partner_row[...], other_row[...]
    last = jnp.where(even, other, partner)
    first = jnp.where(even, partner, other)
    before[:64] = pltpu.roll(last, NE, 1)
    before[64:] = last
    after[:64] = first
    after[64:] = pltpu.roll(first, NE, 1)


def column_kernel(own, one, two, three, columns):
    me = lax.axis_index("lev")
    for k, part in enumerate((own, one, two, three)):
        for p in range(4):
            columns[p, lev_rows(me ^ k), :] = part[p]


def lev_rows(lev):
    return pl.ds(pl.multiple_of(32 * lev, 32), 32)


def physics_kernel(columns, mask, mixing, _wanted, *rest):
    backs, change = rest[:4], rest[4]
    me = lax.axis_index("lev")
    mix = mixing[...]
    for p in range(4):
        x = columns[p]
        mixed = lax.dot_general(
            mix,
            x,
            (((1,), (0,)), ((), ())),
            precision=lax.Precision.HIGHEST,
            preferred_element_type=jnp.float32,
        )
        heavy = 0.5 * jnp.tanh(mixed) - 0.25 * x
        plain = -0.3 * x / (1.0 + x * x)
        change[p] = jnp.where(mask[p : p + 1, :] == 1, heavy, plain)
        for k in range(4):
            backs[k][p] = change[p, lev_rows(me ^ k), :]


def side_lanes(lane):
    return (lane % NE == 0) | (lane % NE == NE - 1), (lane == 0) | (lane == 127)


def wanted_places(near, edge_of):
    curve = lax.axis_index("curve")
    row0, row63 = rim_rows()
    device = ((near // 128) * 171) // 512
    lane_of = near - E * device
    row_of, along = lane_of // NE, lane_of % NE
    apart = device ^ curve
    k_x, k_y = (apart // 8) % 4, (apart // 2) % 4
    in_merged = jnp.where(
        edge_of % 2 == 1,
        24 * k_y + 12 * (device % 2) + jnp.where(edge_of == 3, 0, 6) + row_of,
        96 + jnp.where(edge_of == 0, 0, NE) + along,
    )
    place = HALF * (apart // 32) + MERGED * k_x + in_merged
    lane = lax.broadcasted_iota(jnp.int32, (1, 128), 1)
    side_lane, at_left = side_lanes(lane)

    def row_place(k, row):
        picked = [
            jnp.where(row // 2 == v, place[k : k + 1, 128 * v : 128 * v + 128], 0) for v in range(3)
        ]
        return picked[0] + picked[1] + picked[2]

    sides = jnp.zeros((1, 128), jnp.int32)
    for v in range(3):
        lanes = slice(128 * v, 128 * v + 128)
        both = jnp.where(at_left, place[3:4, lanes], place[1:2, lanes])
        both = jnp.where(side_lane, both, 0)
        sides = sides + (pltpu.roll(both, 2 * v, 1) if v else both)
    return jnp.concatenate([row_place(0, row0), row_place(2, row63), sides], axis=1)


def change_kernel(base, own, two, three, one, out):
    me = lax.axis_index("lev")
    for k, part in enumerate((own, one, two, three)):
        for p in range(4):
            at = 4 * (me ^ k) + p
            out[at] = base[at] + part[p]


POINT = [[0, 1, 2, 3], [3, 7, 11, 15], [12, 13, 14, 15], [0, 4, 8, 12]]


def edge_of_tile(stepped, k, v):
    return jnp.concatenate([stepped[p, :, 128 * v : 128 * v + 128] for p in POINT[k]], axis=0)


def oriented(values, turn):
    four = [values[32 * t : 32 * t + 32] for t in range(4)]
    return [jnp.where(turn, four[3 - t], four[t]) for t in range(4)]


def rim_masks(v):
    row0, row63 = rim_rows()
    lane = lax.broadcasted_iota(jnp.int32, (1, 128), 1)
    row = 2 * v + lane // NE
    side_lane, at_left = side_lanes(lane)
    return [row == row0, side_lane & ~at_left, row == row63, at_left]


def near_kernel(stepped, before, after, turns, base):
    turned = turns[...] == 1
    backwards = 127 - lax.broadcasted_iota(jnp.int32, (128, 128), 1)

    def flip(values):
        return jnp.take_along_axis(values, backwards, axis=1)

    lower = lax.broadcasted_iota(jnp.int32, (1, 128), 1) < NE
    flipped0 = [flip(edge_of_tile(stepped, 0, v)) for v in range(3)] + [flip(after[...])]
    flipped2 = [flip(before[...])] + [flip(edge_of_tile(stepped, 2, v)) for v in range(3)]
    for v in range(3):
        lanes = slice(128 * v, 128 * v + 128)
        own = [edge_of_tile(stepped, k, v) for k in range(4)]
        to_next = [pltpu.roll(own[k], 127, 1) for k in (1, 3)]
        to_last = [pltpu.roll(own[k], 1, 1) for k in (1, 3)]
        across = [
            jnp.where(lower, flipped2[v], flipped2[v + 1]),
            jnp.where(lower, to_next[1], to_last[1]),
            jnp.where(lower, flipped0[v], flipped0[v + 1]),
            jnp.where(lower, to_last[0], to_next[0]),
        ]
        total = [stepped[p, :, lanes] for p in range(16)]
        far = rim_masks(v)
        for k in range(4):
            theirs = oriented(across[k], turned[k : k + 1, lanes])
            for t in range(4):
                p = POINT[k][t]
                term = 0.5 * (theirs[t] - own[k][32 * t : 32 * t + 32])
                total[p] = total[p] + jnp.where(far[k], 0.0, term)
        for p in range(16):
            base[p, :, lanes] = total[p]


def pick_kernel(own, one, both, three, wanted, partner_wanted, mine, theirs):
    curve = lax.axis_index("curve")
    pools = own, one, both.at[1 - (curve // 16) % 2], three
    want = jnp.concatenate([wanted[...], partner_wanted[...]], axis=1)
    found = None
    for k, pool in enumerate(pools):
        at = lax.broadcasted_iota(jnp.int32, (MERGED, 2 * E), 0) + (MERGED * k + HALF * (curve % 2))
        part = exact_dot((at == want).astype(jnp.bfloat16), pool[...], TN)
        found = part if found is None else found + part
    mine[...] = found[:, :E]
    theirs[...] = found[:, E:]


def edge_kernel(stepped, changed, mine, theirs, turns, out, held, sems):
    turned = turns[...] == 1
    found = mine[...] + theirs[...]
    found0, found2, found_side = found[:, :128], found[:, 128:256], found[:, 256:]
    copies = []
    for v in range(3):
        lanes = slice(128 * v, 128 * v + 128)
        back = pltpu.roll(found_side, (128 - 2 * v) % 128, 1) if v else found_side
        total = [changed[p, :, lanes] for p in range(16)]
        far = rim_masks(v)
        for k, across in enumerate((found0, back, found2, back)):
            own = edge_of_tile(stepped, k, v)
            theirs = oriented(across, turned[k : k + 1, lanes])
            for t in range(4):
                p = POINT[k][t]
                term = 0.5 * (theirs[t] - own[32 * t : 32 * t + 32])
                total[p] = total[p] + jnp.where(far[k], term, 0.0)
        for p in range(16):
            held[v, pl.ds(p, 32, stride=16), :] = total[p]
        copies.append(
            pltpu.make_async_copy(held.at[v], out.at[:, pl.ds(128 * v, 128)], sems.at[v])
        )
        copies[-1].start()
    for copy in copies:
        copy.wait()


def on_device(state, wind_x, wind_y, neighbor, neighbor_edge, reversed_edge, branch_mask, mixing):
    flat = state.reshape(512, E)
    part = f32((4, 32, E))
    flat_block, part_block = lane_blocks(512), lane_blocks(4, 32)

    def swap(array, axis, bits):
        devices = lax.axis_size(axis)
        return lax.ppermute(array, axis, [(i, i ^ bits) for i in range(devices)])

    sends = lane_call(split_kernel, (part,) * 4, [flat_block], (part_block,) * 4)(flat)
    cells = [swap(sends[k], "lev", k) for k in (1, 2, 3)]
    stepped, contrib, to_partner, to_other = lane_call(
        step_kernel,
        (
            f32((16, 32, E)),
            f32((CONTRIB, 128)),
            f32((64, 128)),
            f32((64, 128)),
        ),
        [flat_block] * 3 + [whole(4, 32, E)],
        (whole(16, 32, E), whole(CONTRIB, 128), whole(64, 128), whole(64, 128)),
    )(
        flat,
        wind_x.reshape(512, E),
        wind_y.reshape(512, E),
        sends[0],
    )
    inner = [(i, i + 1) for i in range(1, 62, 2) if i != 31]
    other_row = lax.ppermute(to_other, "curve", inner + [(j, i) for i, j in inner])
    partner_row = swap(to_partner, "curve", 1)
    paired = call(pair_kernel, f32((PAIRED, 128)), 4)(
        contrib, swap(contrib, "curve", 1), partner_row, cells[0]
    )
    along_y = [swap(paired, "curve", k << 1) for k in (1, 2, 3)]
    table = jax.ShapeDtypeStruct((4, E), jnp.int32)
    merged, wanted, turns, mask, mix = call(
        merge_kernel,
        (
            f32((MERGED, 128)),
            jax.ShapeDtypeStruct((1, E), jnp.int32),
            table,
            table,
            f32((128, 128)),
        ),
        9,
    )(paired, *along_y, neighbor, neighbor_edge, reversed_edge, branch_mask, mixing)
    partner_wanted = swap(wanted, "curve", 1)
    other_half = lax.ppermute(
        merged,
        "curve",
        [(i, i ^ 32) for i in range(1, 64, 2)],
    )
    long = pl.CostEstimate(flops=10**11, bytes_accessed=10**8, transcendentals=0)
    columns = call(column_kernel, f32((4, 128, E)), 4, cost=long)(sends[0], *cells)
    backs = call(
        physics_kernel, (part,) * 4, 4, [pltpu.VMEM((4, 128, E), jnp.float32)]
    )(columns, mask, mix, partner_wanted)
    changes = [swap(backs[k], "lev", k) for k in (2, 3, 1)]
    piece, twice, before, after = call(
        join_kernel,
        (f32((MERGED, 128)), f32((2, MERGED, 128)), f32((128, 128)), f32((128, 128))),
        4,
        cost=long,
    )(merged, other_half, partner_row, other_row)
    along_x = [swap(piece, "curve", k << 3) for k in (1, 3)]
    groups = [[i, i ^ 16] for i in range(64) if not i & 16]
    across_x = lax.all_to_all(twice, "curve", 0, 0, axis_index_groups=groups, tiled=True)
    base = call(near_kernel, f32((16, 32, E)), 4)(stepped, before, after, turns)
    changed = call(change_kernel, f32((16, 32, E)), 5, cost=long)(base, backs[0], *changes)
    mine, theirs = call(pick_kernel, (f32((128, E)), f32((128, E))), 6)(
        piece, along_x[0], across_x, along_x[1], wanted, partner_wanted
    )
    out = call(
        edge_kernel,
        f32((512, E)),
        5,
        [pltpu.VMEM((3, 512, 128), jnp.float32), pltpu.SemaphoreType.DMA((3,))],
        out_spec=pl.BlockSpec(memory_space=pl.ANY),
    )(stepped, changed, mine, swap(theirs, "curve", 1), turns)
    return out.reshape(32, 16, E)


def solution(mesh):
    in_specs = (
        P("lev", None, "curve"),
        P("lev", None, "curve"),
        P("lev", None, "curve"),
        P(None, "curve"),
        P(None, "curve"),
        P(None, "curve"),
        P("lev", "curve"),
        P(),
    )
    out_specs = P("lev", None, "curve")
    return jax.shard_map(
        on_device, mesh=mesh, in_specs=in_specs, out_specs=out_specs, check_vma=False
    )
```

```python
import functools
import math

import jax
import jax.numpy as jnp
import numpy as np
from jax import lax
from jax.experimental import pallas as pl
from jax.experimental.pallas import tpu as pltpu
from jax.sharding import PartitionSpec as P

NE = 64
ROWS = 6
E = ROWS * NE
CONTRIB = 144
PAIRED = 152
MERGED = 224
HALF = 4 * MERGED
VMEM = pl.BlockSpec(memory_space=pltpu.VMEM)
ANY = pl.BlockSpec(memory_space=pl.ANY)
LIMIT = 24 * 1024 * 1024
NT = (((1,), (1,)), ((), ()))
TN = (((0,), (0,)), ((), ()))


def derivative_table():
    nodes = np.array([-1.0, -1.0 / math.sqrt(5.0), 1.0 / math.sqrt(5.0), 1.0])
    weights = np.array(
        [1.0 / np.prod([nodes[j] - nodes[m] for m in range(4) if m != j]) for j in range(4)]
    )
    table = np.zeros((4, 4))
    for i in range(4):
        for j in range(4):
            if i == j:
                table[i, j] = sum((1.0 / (nodes[i] - nodes[m]) for m in range(4) if m != i))
            else:
                table[i, j] = weights[j] / weights[i] / (nodes[i] - nodes[j])
    table[1, 1] = table[2, 2] = 0.0
    return table


DERIV = derivative_table()


def f32(shape):
    return jax.ShapeDtypeStruct(shape, jnp.float32)


def call(kernel, out_shape, n_in, scratch=(), out_spec=VMEM, cost=None):
    return pl.pallas_call(
        kernel,
        out_shape=out_shape,
        in_specs=[VMEM] * n_in,
        out_specs=jax.tree.map(lambda _: out_spec, out_shape),
        scratch_shapes=list(scratch),
        compiler_params=pltpu.CompilerParams(vmem_limit_bytes=LIMIT),
        cost_estimate=cost,
    )


def lane_blocks(*leading):
    return pl.BlockSpec((*leading, 128), lambda c: (0,) * len(leading) + (c,))


def whole(*shape):
    return pl.BlockSpec(shape, lambda c: (0,) * len(shape))


def lane_call(kernel, out_shape, in_specs, out_specs):
    return pl.pallas_call(
        kernel,
        grid=(3,),
        out_shape=out_shape,
        in_specs=in_specs,
        out_specs=out_specs,
        compiler_params=pltpu.CompilerParams(vmem_limit_bytes=LIMIT),
    )


def split_kernel(state, *sends):
    me = lax.axis_index("lev")
    for k in range(4):
        first = 4 * (me ^ k)
        for p in range(4):
            sends[k][p] = state[pl.ds(first + p, 32, stride=16), :]


def rim_rows():
    start = lax.axis_index("curve") * ROWS
    return (NE - lax.rem(start, NE)) % NE, NE - 1 - lax.rem(start, NE)


def exact_dot(selector, values, dims):
    high = values.astype(jnp.bfloat16)
    rest = values - high.astype(jnp.float32)
    middle = rest.astype(jnp.bfloat16)
    low = (rest - middle.astype(jnp.float32)).astype(jnp.bfloat16)
    out = None
    for part in (low, middle, high):
        args = (selector, part) if dims == NT else (part, selector)
        term = lax.dot_general(*args, dims, preferred_element_type=jnp.float32)
        out = term if out is None else out + term
    return out


def step_kernel(
    state,
    wind_x,
    wind_y,
    _sent,
    stepped,
    contrib,
    to_other,
):
    step = pl.program_id(0)
    lanes = pl.ds(pl.multiple_of(128 * step, 128), 128)
    for tile in range(4):
        at = [pl.ds(128 * tile + p, 8, stride=16) for p in range(16)]
        x = [state[at[p], :] for p in range(16)]
        for a in range(4):
            for b in range(4):
                p = 4 * a + b
                dxi = sum(float(DERIV[a, i]) * x[4 * i + b] for i in range(4) if DERIV[a, i])
                deta = sum(float(DERIV[b, j]) * x[4 * a + j] for j in range(4) if DERIV[b, j])
                moved = wind_x[at[p], :] * dxi + wind_y[at[p], :] * deta
                stepped[p, 8 * tile : 8 * tile + 8, lanes] = x[p] - 0.05 * moved

    @pl.when(step == 2)
    def _():
        take_edges(stepped, contrib, to_other)


def take_edges(stepped, contrib, to_other):
    edge = [
        stepped[0:4].reshape(128, E),
        jnp.concatenate([stepped[4 * t + 3] for t in range(4)], axis=0),
        stepped[12:16].reshape(128, E),
        jnp.concatenate([stepped[4 * t] for t in range(4)], axis=0),
    ]
    last, first = edge[2][:, 256:], edge[0][:, :128]
    low = lax.broadcasted_iota(jnp.int32, (64, 128), 1) < NE
    last = jnp.where(low, pltpu.roll(last[:64], NE, 1), last[64:])
    first = jnp.where(low, first[:64], pltpu.roll(first[64:], NE, 1))
    even = lax.axis_index("curve") % 2 == 0
    contrib[CONTRIB:] = jnp.where(even, last, first)
    to_other[...] = jnp.where(even, first, last)
    row0, row63 = rim_rows()
    r = lax.broadcasted_iota(jnp.int32, (8, E), 0)
    lane = lax.broadcasted_iota(jnp.int32, (8, E), 1)
    odd = r % 2
    left = ((lane == NE * r + (NE - 1) * odd) & (r < ROWS)).astype(jnp.bfloat16)
    right = ((lane == NE * r + (NE - 1) * (1 - odd)) & (r < ROWS)).astype(jnp.bfloat16)
    contrib[0:6] = exact_dot(left, edge[3], NT)[0:6]
    contrib[6:12] = exact_dot(right, edge[1], NT)[0:6]
    r = lax.broadcasted_iota(jnp.int32, (NE, E), 0)
    lane = lax.broadcasted_iota(jnp.int32, (NE, E), 1)
    contrib[12:76] = exact_dot((lane == NE * row0 + r).astype(jnp.bfloat16), edge[0], NT)
    contrib[76:140] = exact_dot((lane == NE * row63 + r).astype(jnp.bfloat16), edge[2], NT)
    contrib[140:CONTRIB] = jnp.zeros((CONTRIB - 140, 128), jnp.float32)


def pair_kernel(a, b, _one, out):
    even = lax.axis_index("curve") % 2 == 0
    out[0:12] = jnp.where(even, a[0:12], b[0:12])
    out[12:24] = jnp.where(even, b[0:12], a[0:12])
    out[24:152] = a[12:140] + b[12:140]


def merge_kernel(a, b, c, d, near, edge_of, turns, mask, mixing, *outs):
    out, wanted, turns_out, mask_out, mixing_out = outs
    wanted[...] = wanted_places(near[...], edge_of[...])
    turns_out[...] = turns[...]
    mask_out[...] = mask[...]
    mixing_out[...] = mixing[...]
    for k, part in enumerate((a, b, c, d)):
        out[24 * k : 24 * k + 24] = part[0:24]
    out[96:224] = (a[24:152] + b[24:152]) + (c[24:152] + d[24:152])


def join_kernel(mine, theirs, partner_row, other_row, out, both, before, after):
    half = jnp.where(lax.axis_index("curve") % 2 == 0, mine[...], theirs[...])
    out[...] = half
    for k in range(2):
        both[k] = half
    even = lax.axis_index("curve") % 2 == 0
    partner, other = partner_row[CONTRIB:], other_row[...]
    last = jnp.where(even, other, partner)
    first = jnp.where(even, partner, other)
    before[:64] = pltpu.roll(last, NE, 1)
    before[64:] = last
    after[:64] = first
    after[64:] = pltpu.roll(first, NE, 1)


def column_kernel(own, one, two, three, columns):
    me = lax.axis_index("lev")
    for k, part in enumerate((own, one, two, three)):
        for p in range(4):
            columns[p, lev_rows(me ^ k), :] = part[p]


def lev_rows(lev):
    return pl.ds(pl.multiple_of(32 * lev, 32), 32)


def physics_kernel(columns, mask, mixing, _wanted, *rest):
    backs, change = rest[:4], rest[4]
    me = lax.axis_index("lev")
    mix = mixing[...]
    for p in range(4):
        x = columns[p]
        mixed = lax.dot_general(
            mix,
            x,
            (((1,), (0,)), ((), ())),
            precision=lax.Precision.HIGHEST,
            preferred_element_type=jnp.float32,
        )
        heavy = 0.5 * jnp.tanh(mixed) - 0.25 * x
        plain = -0.3 * x / (1.0 + x * x)
        change[p] = jnp.where(mask[p : p + 1, :] == 1, heavy, plain)
        for k in range(4):
            backs[k][p] = change[p, lev_rows(me ^ k), :]


def side_lanes(lane):
    return (lane % NE == 0) | (lane % NE == NE - 1), (lane == 0) | (lane == 127)


def wanted_places(near, edge_of):
    curve = lax.axis_index("curve")
    row0, row63 = rim_rows()
    device = ((near // 128) * 171) // 512
    lane_of = near - E * device
    row_of, along = lane_of // NE, lane_of % NE
    apart = device ^ curve
    k_x, k_y = (apart // 8) % 4, (apart // 2) % 4
    in_merged = jnp.where(
        edge_of % 2 == 1,
        24 * k_y + 12 * (device % 2) + jnp.where(edge_of == 3, 0, 6) + row_of,
        96 + jnp.where(edge_of == 0, 0, NE) + along,
    )
    place = HALF * (apart // 32) + MERGED * k_x + in_merged
    lane = lax.broadcasted_iota(jnp.int32, (1, 128), 1)
    side_lane, at_left = side_lanes(lane)

    def row_place(k, row):
        picked = [
            jnp.where(row // 2 == v, place[k : k + 1, 128 * v : 128 * v + 128], 0) for v in range(3)
        ]
        return picked[0] + picked[1] + picked[2]

    sides = jnp.zeros((1, 128), jnp.int32)
    for v in range(3):
        lanes = slice(128 * v, 128 * v + 128)
        both = jnp.where(at_left, place[3:4, lanes], place[1:2, lanes])
        both = jnp.where(side_lane, both, 0)
        sides = sides + (pltpu.roll(both, 2 * v, 1) if v else both)
    return jnp.concatenate([row_place(0, row0), row_place(2, row63), sides], axis=1)


def change_kernel(base, own, two, three, one, out):
    me = lax.axis_index("lev")
    for k, part in ((0, own), (2, two), (3, three), (1, one)):
        rows = pl.ds(4 * (me ^ k), 4)
        out[rows] = base[rows] + part[...]


POINT = [[0, 1, 2, 3], [3, 7, 11, 15], [12, 13, 14, 15], [0, 4, 8, 12]]


def edge_of_tile(stepped, k, v):
    return jnp.concatenate([stepped[p, :, 128 * v : 128 * v + 128] for p in POINT[k]], axis=0)


def oriented(values, turn):
    four = [values[32 * t : 32 * t + 32] for t in range(4)]
    return [jnp.where(turn, four[3 - t], four[t]) for t in range(4)]


def rim_masks(v):
    row0, row63 = rim_rows()
    lane = lax.broadcasted_iota(jnp.int32, (1, 128), 1)
    row = 2 * v + lane // NE
    side_lane, at_left = side_lanes(lane)
    return [row == row0, side_lane & ~at_left, row == row63, at_left]


def near_kernel(stepped, before, after, turns, base):
    turned = turns[...] == 1
    backwards = 127 - lax.broadcasted_iota(jnp.int32, (128, 128), 1)

    def flip(values):
        return jnp.take_along_axis(values, backwards, axis=1)

    lower = lax.broadcasted_iota(jnp.int32, (1, 128), 1) < NE
    flipped0 = [flip(edge_of_tile(stepped, 0, v)) for v in range(3)] + [flip(after[...])]
    flipped2 = [flip(before[...])] + [flip(edge_of_tile(stepped, 2, v)) for v in range(3)]
    for v in range(3):
        lanes = slice(128 * v, 128 * v + 128)
        own = [edge_of_tile(stepped, k, v) for k in range(4)]
        to_next = [pltpu.roll(own[k], 127, 1) for k in (1, 3)]
        to_last = [pltpu.roll(own[k], 1, 1) for k in (1, 3)]
        across = [
            jnp.where(lower, flipped2[v], flipped2[v + 1]),
            jnp.where(lower, to_next[1], to_last[1]),
            jnp.where(lower, flipped0[v], flipped0[v + 1]),
            jnp.where(lower, to_last[0], to_next[0]),
        ]
        total = [stepped[p, :, lanes] for p in range(16)]
        far = rim_masks(v)
        for k in range(4):
            theirs = oriented(across[k], turned[k : k + 1, lanes])
            for t in range(4):
                p = POINT[k][t]
                term = 0.5 * (theirs[t] - own[k][32 * t : 32 * t + 32])
                total[p] = total[p] + jnp.where(far[k], 0.0, term)
        for p in range(16):
            base[p, :, lanes] = total[p]


def pick_kernel(own, one, both, three, wanted, partner_wanted, mine, theirs):
    curve = lax.axis_index("curve")
    pools = own, one, both.at[1 - (curve // 16) % 2], three
    want = jnp.concatenate([wanted[...], partner_wanted[...]], axis=1)
    found = None
    for k, pool in enumerate(pools):
        at = lax.broadcasted_iota(jnp.int32, (MERGED, 2 * E), 0) + (MERGED * k + HALF * (curve % 2))
        part = exact_dot((at == want).astype(jnp.bfloat16), pool[...], TN)
        found = part if found is None else found + part
    mine[...] = found[:, :E]
    theirs[...] = found[:, E:]


def edge_kernel(stepped, changed, mine, theirs, turns, out, held, sems):
    turned = turns[...] == 1
    found = mine[...] + theirs[...]
    found0, found2, found_side = found[:, :128], found[:, 128:256], found[:, 256:]
    copies = []
    for v in range(3):
        lanes = slice(128 * v, 128 * v + 128)
        back = pltpu.roll(found_side, (128 - 2 * v) % 128, 1) if v else found_side
        total = [changed[p, :, lanes] for p in range(16)]
        far = rim_masks(v)
        for k, across in enumerate((found0, back, found2, back)):
            own = edge_of_tile(stepped, k, v)
            theirs = oriented(across, turned[k : k + 1, lanes])
            for t in range(4):
                p = POINT[k][t]
                term = 0.5 * (theirs[t] - own[32 * t : 32 * t + 32])
                total[p] = total[p] + jnp.where(far[k], term, 0.0)
        for p in range(16):
            held[v, pl.ds(p, 32, stride=16), :] = total[p]
        copies.append(
            pltpu.make_async_copy(held.at[v], out.at[:, pl.ds(128 * v, 128)], sems.at[v])
        )
        copies[-1].start()
    for copy in copies:
        copy.wait()


def on_device(state, wind_x, wind_y, neighbor, neighbor_edge, reversed_edge, branch_mask, mixing):
    flat = state.reshape(512, E)
    part = f32((4, 32, E))
    flat_block, part_block = lane_blocks(512), lane_blocks(4, 32)

    def swap(array, axis, bits):
        devices = lax.axis_size(axis)
        return lax.ppermute(array, axis, [(i, i ^ bits) for i in range(devices)])

    sends = lane_call(split_kernel, (part,) * 4, [flat_block], (part_block,) * 4)(flat)
    cells = [swap(sends[k], "lev", k) for k in (1, 2, 3)]
    stepped, contrib, to_other = lane_call(
        step_kernel,
        (
            f32((16, 32, E)),
            f32((CONTRIB + 64, 128)),
            f32((64, 128)),
        ),
        [flat_block] * 3 + [whole(4, 32, E)],
        (whole(16, 32, E), whole(CONTRIB + 64, 128), whole(64, 128)),
    )(
        flat,
        wind_x.reshape(512, E),
        wind_y.reshape(512, E),
        sends[0],
    )
    inner = [(i, i + 1) for i in range(1, 62, 2) if i != 31]
    other_row = lax.ppermute(to_other, "curve", inner + [(j, i) for i, j in inner])
    partner = swap(contrib, "curve", 1)
    paired = call(pair_kernel, f32((PAIRED, 128)), 3)(
        contrib, partner, cells[0]
    )
    along_y = [swap(paired, "curve", k << 1) for k in (1, 2, 3)]
    table = jax.ShapeDtypeStruct((4, E), jnp.int32)
    merged, wanted, turns, mask, mix = call(
        merge_kernel,
        (
            f32((MERGED, 128)),
            jax.ShapeDtypeStruct((1, E), jnp.int32),
            table,
            table,
            f32((128, 128)),
        ),
        9,
    )(paired, *along_y, neighbor, neighbor_edge, reversed_edge, branch_mask, mixing)
    partner_wanted = swap(wanted, "curve", 1)
    other_half = lax.ppermute(
        merged,
        "curve",
        [(i, i ^ 32) for i in range(1, 64, 2)],
    )
    long = pl.CostEstimate(flops=10**11, bytes_accessed=10**8, transcendentals=0)
    columns = call(column_kernel, f32((4, 128, E)), 4, cost=long)(sends[0], *cells)
    backs = call(
        physics_kernel, (part,) * 4, 4, [pltpu.VMEM((4, 128, E), jnp.float32)]
    )(columns, mask, mix, partner_wanted)
    changes = [swap(backs[k], "lev", k) for k in (2, 3, 1)]
    piece, twice, before, after = call(
        join_kernel,
        (f32((MERGED, 128)), f32((2, MERGED, 128)), f32((128, 128)), f32((128, 128))),
        4,
        cost=long,
    )(merged, other_half, partner, other_row)
    along_x = [swap(piece, "curve", k << 3) for k in (1, 3)]
    groups = [[i, i ^ 16] for i in range(64) if not i & 16]
    across_x = lax.all_to_all(twice, "curve", 0, 0, axis_index_groups=groups, tiled=True)
    base = call(near_kernel, f32((16, 32, E)), 4)(stepped, before, after, turns)
    changed = call(change_kernel, f32((16, 32, E)), 5, cost=long)(base, backs[0], *changes)
    mine, theirs = call(pick_kernel, (f32((128, E)), f32((128, E))), 6)(
        piece, along_x[0], across_x, along_x[1], wanted, partner_wanted
    )
    out = call(
        edge_kernel,
        f32((512, E)),
        5,
        [pltpu.VMEM((3, 512, 128), jnp.float32), pltpu.SemaphoreType.DMA((3,))],
        out_spec=pl.BlockSpec(memory_space=pl.ANY),
    )(stepped, changed, mine, swap(theirs, "curve", 1), turns)
    return out.reshape(32, 16, E)


def solution(mesh):
    in_specs = (
        P("lev", None, "curve"),
        P("lev", None, "curve"),
        P("lev", None, "curve"),
        P(None, "curve"),
        P(None, "curve"),
        P(None, "curve"),
        P("lev", "curve"),
        P(),
    )
    out_specs = P("lev", None, "curve")
    return jax.shard_map(
        on_device, mesh=mesh, in_specs=in_specs, out_specs=out_specs, check_vma=False
    )
```
